128 devices in a mesh: frame: 16 (over y, z), head: 8 (over x, core).
Axes of the slice: x: 4, y: 4, z: 4, core: 2. Of those that a mesh axis runs over, the one named last changes fastest.
Arguments:
- video_q: bfloat16 [16384, 3072], P(('frame', 'head'))
- video_k: bfloat16 [16384, 3072], P(('frame', 'head'))
- video_v: bfloat16 [16384, 3072], P(('frame', 'head')), may hold values from -6 to 6
- text_q: bfloat16 [256, 3072], P(None, 'head')
- text_k: bfloat16 [256, 3072], P(None, 'head'), may hold values from -6 to 6
- text_v: bfloat16 [256, 3072], P(None, 'head'), may hold values from -6 to 6
- block_mask: int32 [128, 128], replicated, may hold values from 0 to 1, as said below
- text_count: int32 [1], replicated, may hold values from 1 to 256
Outputs:
- video_out: bfloat16 [16384, 3072], P(('frame', 'head'))
- text_out: bfloat16 [256, 3072], P(None, 'head')
The draws below stay inside these ranges and needn't reach their ends.
Inputs may be any that keep to these rules, and one draw needn't show every extreme that they name: block_mask is drawn at random with density falling with block distance; block_mask[i, j] is 1 where |i - j| <= 1 and 0 where |i - j| > 32; block_mask[0, 32] is 1.
All inputs are finite; a program needn't handle non-finite values.
Results may differ from the reference program's by a relative error of at most 0.0075.
Values may be sent and summed in bfloat16 or wider, within the bound.
No kernel may reach another device: no remote copies, remote signals or barrier semaphores. Data moves between devices by JAX's collectives and lax.ppermute only.
A program may use at most 64 MiB of HBM per device.

```python
import jax
import jax.numpy as jnp
from jax import lax

H = 24
DH = 128
D = 3072
TOK_DEV = 128
TEXT = 256
BLOCK = 128
TOKENS = 16384
NBLK = 128
REACH = 32
N_FRAME = 16
N_HEAD = 8


def shared_keys(key, near):
    base = jnp.clip(jax.random.normal(key, (TOKENS, D), jnp.float32), -6.0, 6.0)
    noise = jax.random.normal(jax.random.fold_in(key, 77), (TOKENS, D), jnp.float32)
    rows = jnp.arange(TOKENS)[:, None]
    follow = jnp.where(rows % 512 == 101, 1.0, 0.0)
    paired = jnp.roll(base, 1, axis=0) + near * noise
    return base + follow * (paired - base)


def draw_video_k(key, part):
    base = shared_keys(key, 0.1)
    return base.astype(jnp.bfloat16)


def drawn_strength(frac, low, rise):
    return (low + rise * frac) / DH ** 0.5


def draw_video_q(key, part):
    base = shared_keys(key, 0.1)
    low, rise = (100.0, 100.0)
    key = jax.random.fold_in(key, 1)
    values = jnp.clip(jax.random.normal(key, (TOKENS, D), jnp.float32), -6.0, 6.0)
    rows = jnp.arange(TOKENS)[:, None]
    strength = drawn_strength(rows.astype(jnp.float32) / TOKENS, low, rise)
    values = jnp.where(rows % 512 == 100, strength * base, values)
    return values.astype(jnp.bfloat16)


def draw_text_q(key, part):
    base = shared_keys(key, 0.1)
    low, rise = (100.0, 100.0)
    key = jax.random.fold_in(key, 2)
    values = jnp.clip(jax.random.normal(key, (TEXT, D), jnp.float32), -6.0, 6.0)
    rows = jnp.arange(TEXT)
    picked = jnp.take(base, (rows * 512 + 100) % TOKENS, axis=0)
    strength = drawn_strength(rows[:, None].astype(jnp.float32) / TEXT, low, rise)
    values = jnp.where(rows[:, None] % 32 == 5, strength * picked, values)
    return values.astype(jnp.bfloat16)


def draw_block_mask(key, part):
    key = jax.random.fold_in(key, 5)
    rows = jnp.arange(NBLK)[:, None]
    cols = jnp.arange(NBLK)[None, :]
    dist = jnp.abs(rows - cols)
    ticket = jax.random.randint(key, (NBLK, NBLK), 0, 1024)
    keep = (dist <= 1) | (ticket * (8 + dist) < 8 * 1024)
    keep = keep & (dist <= REACH)
    keep = keep | (rows == 0) & (cols == REACH)
    return keep.astype(jnp.int32)


def block_scale(rng, dims, cuts, smallest, top_value):
    def one(position, parts):
        steps = jax.random.uniform(jax.random.fold_in(jax.random.fold_in(rng, 6), position), (parts,), jnp.float32, smallest / len(cuts), top_value / len(cuts))
        return jnp.repeat(jnp.exp(steps), dims[position] // parts).reshape((-1,) + (1,) * (len(dims) - position - 1))

    gain = one(*cuts[0])
    for cut in cuts[1:]:
        gain = gain * one(*cut)
    return gain


def bell_draw(rng, shape, spread, bound, shards=(), kind=jnp.bfloat16):
    drawn = jax.random.normal(rng, shape, jnp.float32) * spread
    if len(shards) > 0:
        drawn = block_scale(rng, shape, shards, -0.22, 0.18) * drawn
    return jnp.clip(drawn, min=-bound, max=bound).astype(kind)


def setup_inputs(seed: int = 0) -> dict:
    splits = jax.random.split(jax.random.key(seed), 9)
    return {
        "video_q": draw_video_q(jax.random.fold_in(splits[8], 71), 0),
        "video_k": draw_video_k(jax.random.fold_in(splits[8], 71), 0),
        "video_v": bell_draw(splits[2], (TOKENS, D), 1.0, 6.0, ((0, 128),)),
        "text_q": draw_text_q(jax.random.fold_in(splits[8], 71), 0),
        "text_k": bell_draw(splits[4], (TEXT, D), 1.0, 6.0, ((1, 8),)),
        "text_v": bell_draw(splits[5], (TEXT, D), 1.0, 6.0, ((1, 8),)),
        "block_mask": draw_block_mask(jax.random.fold_in(splits[8], 71), 0),
        "text_count": jax.random.randint(splits[7], (1,), 1, TEXT + 1).astype(jnp.int32),
    }


neg_fill = -1.0e30


def by_heads(x, rows):
    return x.reshape(rows, H, DH).transpose(1, 0, 2)


def reference(video_q, video_k, video_v, text_q, text_k, text_v, block_mask, text_count):
    scale = DH ** -0.5
    group = TOK_DEV * N_HEAD
    blocks = group // BLOCK
    steps_out = N_FRAME // 4
    span = (2 * steps_out + 1) * group
    live = jnp.arange(TEXT) < text_count[0]
    query_h, key_h, value_h = by_heads(video_q, TOKENS), by_heads(video_k, TOKENS), by_heads(video_v, TOKENS)
    tq_h, tk_h, tv_h = by_heads(text_q, TEXT), by_heads(text_k, TEXT), by_heads(text_v, TEXT)

    def video_group(index):
        head = index // N_FRAME
        frame = index % N_FRAME
        query = lax.dynamic_slice_in_dim(lax.dynamic_index_in_dim(query_h, head, 0, keepdims=False), (frame * group).astype(jnp.int32), group, 0)
        keys_all = lax.dynamic_index_in_dim(key_h, head, 0, keepdims=False)
        values_all = lax.dynamic_index_in_dim(value_h, head, 0, keepdims=False)
        start = jnp.clip((frame - steps_out) * group, 0, TOKENS - span).astype(jnp.int32)
        keys = lax.dynamic_slice_in_dim(keys_all, start, span, 0)
        values = lax.dynamic_slice_in_dim(values_all, start, span, 0)
        mask_rows = lax.dynamic_slice_in_dim(block_mask, (frame * blocks).astype(jnp.int32), blocks, 0)
        mask_cols = lax.dynamic_slice_in_dim(mask_rows, (start // BLOCK).astype(jnp.int32), span // BLOCK, 1)
        keep = jnp.repeat(jnp.repeat(mask_cols > 0, BLOCK, 0), BLOCK, 1)
        text_keys = lax.dynamic_index_in_dim(tk_h, head, 0, keepdims=False)
        text_values = lax.dynamic_index_in_dim(tv_h, head, 0, keepdims=False)
        s_video = jnp.where(keep, jnp.dot(query, keys.T, preferred_element_type=jnp.float32) * scale, neg_fill)
        s_text = jnp.where(live[None, :], jnp.dot(query, text_keys.T, preferred_element_type=jnp.float32) * scale, neg_fill)
        top = jnp.maximum(jnp.max(s_video, axis=1), jnp.max(s_text, axis=1))
        w_video = jnp.where(keep, jnp.exp(s_video - top[:, None]), 0.0)
        w_text = jnp.where(live[None, :], jnp.exp(s_text - top[:, None]), 0.0)
        total = jnp.sum(w_video, axis=1) + jnp.sum(w_text, axis=1)
        summed = jnp.dot(w_video.astype(jnp.bfloat16), values, preferred_element_type=jnp.float32)
        summed = summed + jnp.dot(w_text.astype(jnp.bfloat16), text_values, preferred_element_type=jnp.float32)
        return (summed / total[:, None]).astype(jnp.bfloat16)

    video_parts = lax.map(video_group, jnp.arange(H * N_FRAME, dtype=jnp.int32))
    video_out = video_parts.reshape(H, N_FRAME, group, DH).transpose(1, 2, 0, 3).reshape(TOKENS, D)

    def text_head(operands):
        query, keys, values, text_keys, text_values = operands
        s_video = jnp.dot(query, keys.T, preferred_element_type=jnp.float32) * scale
        s_text = jnp.where(live[None, :], jnp.dot(query, text_keys.T, preferred_element_type=jnp.float32) * scale, neg_fill)
        top = jnp.maximum(jnp.max(s_video, axis=1), jnp.max(s_text, axis=1))
        w_video = jnp.exp(s_video - top[:, None])
        w_text = jnp.where(live[None, :], jnp.exp(s_text - top[:, None]), 0.0)
        total = jnp.sum(w_video, axis=1) + jnp.sum(w_text, axis=1)
        summed = jnp.dot(w_video.astype(jnp.bfloat16), values, preferred_element_type=jnp.float32)
        summed = summed + jnp.dot(w_text.astype(jnp.bfloat16), text_values, preferred_element_type=jnp.float32)
        return (summed / total[:, None]).astype(jnp.bfloat16)

    text_parts = lax.map(text_head, (tq_h, key_h, value_h, tk_h, tv_h))
    text_out = text_parts.transpose(1, 0, 2).reshape(TEXT, D)
    return video_out, text_out
```

```python
import functools

import jax
import jax.numpy as jnp
import numpy as np
from jax import lax
from jax.experimental import pallas as pl
from jax.experimental.pallas import tpu as pltpu
from jax.sharding import Mesh, PartitionSpec as P

DH = 128
TEXT = 256
BLOCK = 128
SLAB = 32
HALF = 16
NTQ = 2
REC = 384
QREC = 256
OREC = 272
STEP = 4
UNROLL = 4
LOG2 = float(DH**-0.5 * np.log2(np.e))
neg_fill = -1e30
FLAG = 4096
FIRST_LEN = SLAB * STEP
REST_LEN = SLAB * (HALF + STEP) + 4 * STEP
HALO_LEN = HALF * (2 * HALF + STEP) + 4 * STEP

VM = pl.BlockSpec(memory_space=pltpu.VMEM)
SM = pl.BlockSpec(memory_space=pltpu.SMEM)
ANY = pl.BlockSpec(memory_space=pl.ANY)
PARAMS = pltpu.CompilerParams(vmem_limit_bytes=20 << 20)


def head_a(chip):
    z, x = chip // 4, chip % 4
    return 6 * x + 3 * (z // 2) + z % 2


def head_c(chip):
    z, x = chip // 4, chip % 4
    return 6 * x + 3 * (z // 2) + 2


def packed(vt, half):
    cols = vt[:, 64 * half : 64 * half + 64]
    return jnp.concatenate([cols[:64], cols[64:]], axis=1)


def prep_kv_kernel(k_hbm, v_hbm, out_ref, k_ref, v_ref, sems):
    third = 8 * DH
    copies = [
        [
            pltpu.make_async_copy(
                hbm.at[:, pl.ds(third * i, third)], ref.at[:, pl.ds(third * i, third)], sems.at[2 * i + j]
            )
            for j, (hbm, ref) in enumerate(((k_hbm, k_ref), (v_hbm, v_ref)))
        ]
        for i in range(3)
    ]
    for pair in copies:
        for copy in pair:
            copy.start()
    arrived = 0
    for x in range(4):
        while 8 * arrived < 6 * (x + 1):
            for copy in copies[arrived]:
                copy.wait()
            arrived += 1
        for z in range(4):
            chip = 4 * z + x
            a, c, half = head_a(chip) * DH, head_c(chip) * DH, z % 2
            out_ref[chip, 0:128] = k_ref[:, a : a + DH]
            out_ref[chip, 128:192] = k_ref[64 * half : 64 * half + 64, c : c + DH]
            out_ref[chip, 192:320] = v_ref[:, a : a + DH].T
            out_ref[chip, 320:384] = packed(v_ref[:, c : c + DH].T, half)


def prep_q_kernel(q_ref, out_ref):
    for chip in range(16):
        a, c = head_a(chip) * DH, head_c(chip) * DH
        out_ref[chip, 0:128] = q_ref[:, a : a + DH].T
        out_ref[chip, 128:256] = q_ref[:, c : c + DH].T


def lists_kernel(place_ref, mask_ref, first_ref, rest_ref, halo_a_ref, halo_b_ref, n_ref):
    y, c = place_ref[0], place_ref[1]

    def kept(q, j, dy):
        col = (y + dy) * SLAB + 2 * j + c
        inside = jnp.logical_and(col >= 0, col < 4 * SLAB)
        value = mask_ref[y * SLAB + q, jnp.clip(col, 0, 4 * SLAB - 1)]
        return jnp.where(inside, value, 0)

    def row_of(n):
        return jnp.where(n < HALF, 2 * n + c, 2 * (n - HALF) + 1 - c)

    def close(ref, start, pos, size):
        last = ref[jnp.maximum(pos - 1, 0)]
        for _ in range(size - 1):
            missing = (pos - start) % size != 0

            @pl.when(missing)
            def _():
                ref[pos] = last | FLAG

            pos = pos + jnp.where(missing, 1, 0)
        return pos

    def own(n, pos):
        row = row_of(n)
        count = jnp.int32(0)
        start = pos
        for j in range(HALF):
            hit = kept(row, j, 0)

            @pl.when(jnp.logical_and(hit > 0, count < STEP - 1))
            def _():
                first_ref[n * STEP + count] = n * 64 + j

            @pl.when(jnp.logical_and(hit > 0, count >= STEP - 1))
            def _():
                rest_ref[pos] = n * 64 + j

            pos = pos + jnp.where(jnp.logical_and(hit > 0, count >= STEP - 1), 1, 0)
            count = count + hit
        some = jnp.minimum(count, STEP - 1)
        last = jnp.where(some > 0, first_ref[n * STEP + jnp.maximum(some - 1, 0)], n * 64)
        for k in range(STEP):

            @pl.when(k >= some)
            def _():
                first_ref[n * STEP + k] = last | FLAG

        return close(rest_ref, start, pos, STEP)

    end = lax.fori_loop(0, SLAB, own, jnp.int32(0))
    n_ref[0] = end // STEP
    for k in range(4 * STEP):
        rest_ref[end + k] = FLAG
    for which, (ref, base) in enumerate(((halo_a_ref, HALF), (halo_b_ref, 0))):

        def far(n, pos):
            start = pos
            row = row_of(n + base)
            for dy, shift in ((-1, 0), (1, HALF)):
                for j in range(HALF):
                    hit = kept(row, j, dy)

                    @pl.when(hit > 0)
                    def _():
                        ref[pos] = n * 64 + shift + j

                    pos = pos + hit
            return close(ref, start, pos, STEP)

        end = lax.fori_loop(0, HALF, far, jnp.int32(0))
        n_ref[1 + which] = end // STEP
        for k in range(4 * STEP):
            ref[end + k] = FLAG
    n_ref[3] = 0


def fold(x, op):
    return op(x.reshape(-1, 8, DH), axis=0)


def slots(list_ref, t):
    codes = [list_ref[STEP * t + k] for k in range(STEP)]
    q = (codes[0] & (FLAG - 1)) >> 6
    gaps = [jnp.where(code >= FLAG, jnp.float32(1e30), jnp.float32(0)) for code in codes]
    return q, [code & 63 for code in codes], gaps


def wide_c(kv_ref, js):
    low, high = [], []
    for j in js:
        part = kv_ref[j, 320:384]
        low.append(part[:, :64])
        high.append(part[:, 64:])
    return jnp.concatenate([jnp.concatenate(low, axis=1), jnp.concatenate(high, axis=1)], axis=0)


def scores(kv_ref, q_ref, s_ref, t_ref, buf, q, js, live=None):
    for h, (low, size, row) in enumerate(((0, 128, 0), (512, 64, 128))):
        keys = jnp.concatenate([kv_ref[j, row : row + size] for j in js], axis=0)
        s = jnp.dot(keys, q_ref[q, 128 * h : 128 * h + 128], preferred_element_type=jnp.float32)
        if live is not None:
            rows = lax.broadcasted_iota(jnp.int32, (size, DH), 0)
            s = jnp.concatenate([jnp.where(rows < live[h], s[:size], neg_fill), s[size:]], axis=0)
        s_ref[buf, low : low + STEP * size] = s
        t_ref[buf, h] = jnp.broadcast_to(column_max(s), (8, DH))


def column_max(s):
    return jnp.max(fold(s, jnp.max), axis=0, keepdims=True)


def weights(parts, top, gaps):
    return [jnp.exp2((s - (top + gap)) * LOG2) for s, gap in zip(parts, gaps)]


def values_of(kv_ref, js, h):
    if h == 0:
        return jnp.concatenate([kv_ref[j, 192:320] for j in js], axis=1)
    return wide_c(kv_ref, js)


def parts_of(s_ref, buf, h):
    low, size = (0, 128) if h == 0 else (512, 64)
    return [s_ref[buf, low + size * k : low + size * (k + 1)] for k in range(STEP)]


def first_step(kv_ref, s_ref, t_ref, acc_ref, m_ref, l_ref, buf, q, js, gaps):
    for h in range(2):
        top = t_ref[buf, h]
        w = weights(parts_of(s_ref, buf, h), top[:1], gaps)
        m_ref[q, h] = top
        l_ref[q, h] = sum(fold(x, jnp.sum) for x in w)
        w = jnp.concatenate(w, axis=0).astype(jnp.bfloat16)
        acc_ref[q, h] = jnp.dot(values_of(kv_ref, js, h), w, preferred_element_type=jnp.float32)


def next_step(kv_ref, s_ref, t_ref, acc_ref, m_ref, l_ref, buf, q, js, gaps):
    for h in range(2):
        old = m_ref[q, h]
        new = jnp.maximum(old, t_ref[buf, h])
        factor = jnp.exp2((old - new) * LOG2)
        w = weights(parts_of(s_ref, buf, h), new[:1], gaps)
        m_ref[q, h] = new
        l_ref[q, h] = l_ref[q, h] * factor + sum(fold(x, jnp.sum) for x in w)
        w = jnp.concatenate(w, axis=0).astype(jnp.bfloat16)
        acc_ref[q, h] = acc_ref[q, h] * factor[:1] + jnp.dot(
            values_of(kv_ref, js, h), w, preferred_element_type=jnp.float32
        )


def run_list(kv_ref, q_ref, s_ref, t_ref, acc_ref, m_ref, l_ref, list_ref, steps):
    def score(t, buf):
        q, js, _ = slots(list_ref, t)
        scores(kv_ref, q_ref, s_ref, t_ref, buf, q, js)

    def step(t, buf):
        q, js, gaps = slots(list_ref, t)
        next_step(kv_ref, s_ref, t_ref, acc_ref, m_ref, l_ref, buf, q, js, gaps)

    score(0, 0)

    def body(i, carry):
        for k in range(UNROLL):
            score(UNROLL * i + k + 1, (k + 1) % 2)
            step(UNROLL * i + k, k % 2)
        return carry

    lax.fori_loop(0, steps // UNROLL, body, 0)

    def rest(i, carry):
        @pl.when(i % 2 == 0)
        def _():
            score(i + 1, 1)
            step(i, 0)

        @pl.when(i % 2 == 1)
        def _():
            score(i + 1, 0)
            step(i, 1)

        return carry

    lax.fori_loop(steps // UNROLL * UNROLL, steps, rest, 0)


def own_kernel(
    first_ref, rest_ref, n_ref, live_ref, kv_hbm, text_hbm, q_hbm, other_hbm,
    acc_ref, m_ref, l_ref, kv_ref, q_ref, s_ref, t_ref, sems,
):
    copies = [
        pltpu.make_async_copy(kv_hbm, kv_ref.at[pl.ds(0, HALF)], sems.at[0]),
        pltpu.make_async_copy(text_hbm, kv_ref.at[pl.ds(HALF, 1)], sems.at[1]),
        pltpu.make_async_copy(q_hbm, q_ref.at[pl.ds(0, HALF)], sems.at[2]),
        pltpu.make_async_copy(other_hbm, q_ref.at[pl.ds(HALF, HALF)], sems.at[3]),
    ]
    for copy in copies:
        copy.start()
    for copy in copies:
        copy.wait()

    def line(n):
        codes = [first_ref[STEP * n + k] for k in range(STEP - 1)]
        gaps = [jnp.float32(0)]
        gaps += [jnp.where(code >= FLAG, jnp.float32(1e30), jnp.float32(0)) for code in codes]
        return [jnp.int32(HALF)] + [code & 63 for code in codes], gaps

    def score(n, buf):
        live = (live_ref[0], live_ref[1])
        scores(kv_ref, q_ref, s_ref, t_ref, buf, n, line(n)[0], live)

    def step(n, buf):
        js, gaps = line(n)
        first_step(kv_ref, s_ref, t_ref, acc_ref, m_ref, l_ref, buf, n, js, gaps)

    score(0, 0)

    def body(i, carry):
        for k in range(UNROLL):
            score(jnp.minimum(UNROLL * i + k + 1, SLAB - 1), (k + 1) % 2)
            step(UNROLL * i + k, k % 2)
        return carry

    lax.fori_loop(0, SLAB // UNROLL, body, 0)
    run_list(kv_ref, q_ref, s_ref, t_ref, acc_ref, m_ref, l_ref, rest_ref, n_ref[0])


def text_kernel(live_ref, kv_ref, text_ref, q_ref, out_ref, s_ref, t_ref, acc_ref, m_ref, l_ref):
    none = [jnp.float32(0)] * STEP
    live = (live_ref[2], live_ref[3])

    def one(block, carry):
        for start in range(0, HALF, STEP):
            js = list(range(start, start + STEP))
            scores(kv_ref, q_ref, s_ref, t_ref, 0, block, js)
            step = next_step if start else first_step
            step(kv_ref, s_ref, t_ref, acc_ref, m_ref, l_ref, 0, block, js, none)
        for h, (low, size, row) in enumerate(((0, 128, 0), (512, 64, 128))):
            s = jnp.dot(
                text_ref[0, row : row + size],
                q_ref[block, 128 * h : 128 * h + 128],
                preferred_element_type=jnp.float32,
            )
            rows = lax.broadcasted_iota(jnp.int32, s.shape, 0)
            s = jnp.where(rows < live[h], s, neg_fill)
            old = m_ref[block, h]
            new = jnp.maximum(old, column_max(s))
            factor = jnp.exp2((old - new) * LOG2)
            w = jnp.exp2((s - new[:1]) * LOG2)
            total = row_sum(l_ref[block, h] * factor) + row_sum(fold(w, jnp.sum))
            v = text_ref[0, 192:320] if h == 0 else wide_c(text_ref, [0])
            acc = acc_ref[block, h] * factor[:1] + jnp.dot(
                v, w.astype(jnp.bfloat16), preferred_element_type=jnp.float32
            )
            put_text(out_ref, h * NTQ + block, new[:1], total, acc)
        return carry

    lax.fori_loop(0, NTQ, one, 0)


def row_sum(x):
    return jnp.sum(x, axis=0, keepdims=True)


def put_text(ref, at, top, total, acc):
    ref[at, 0:128] = acc.astype(jnp.bfloat16)
    ref[at, 128:144] = stat_rows([top, total])


def merged(blocks):
    stats = [stats_of(block[128:144], 2) for block in blocks]
    top = functools.reduce(jnp.maximum, [s[0] for s in stats])
    factors = [jnp.exp2((s[0] - top) * LOG2) for s in stats]
    total = sum(s[1] * f for s, f in zip(stats, factors))
    return top, total, sum(b[0:128].astype(jnp.float32) * f for b, f in zip(blocks, factors))


def merge_text_kernel(mine_ref, other_ref, out_ref):
    for block in range(NTQ):
        for head in range(3):
            at = (0 if head < 2 else NTQ) + block
            members = (head,) if head < 2 else (0, 1)
            blocks = [ref[i, at] for ref in (mine_ref, other_ref) for i in members]
            put_text(out_ref, head * NTQ + block, *merged(blocks))


def final_text_kernel(*refs):
    for block in range(NTQ):
        for head in range(3):
            _, total, acc = merged([ref[head * NTQ + block] for ref in refs[:-1]])
            out = (acc / total).astype(jnp.bfloat16).T
            refs[-1][128 * block : 128 * block + 128, head * DH : head * DH + DH] = out


def split3(x):
    rows = []
    for _ in range(3):
        part = x.astype(jnp.bfloat16)
        rows.append(part)
        x = x - part.astype(jnp.float32)
    return rows


def stat_rows(rows):
    parts = [part for row in rows for part in split3(row)]
    pad = jnp.zeros((16 - len(parts), DH), jnp.bfloat16)
    return jnp.concatenate(parts + [pad], axis=0)


def stats_of(block, count):
    x = block.astype(jnp.float32)
    return [x[3 * i : 3 * i + 1] + x[3 * i + 1 : 3 * i + 2] + x[3 * i + 2 : 3 * i + 3] for i in range(count)]


def halo_kernel(
    which, list_ref, n_ref, down_hbm, up_hbm, q_hbm, acc_hbm, m_hbm, l_hbm,
    *refs,
):
    if which == 0:
        out_ref, kv_ref, q_ref, s_ref, t_ref, acc_ref, m_ref, l_ref, sems = refs
    else:
        acc_ref, m_ref, l_ref, kv_ref, q_ref, s_ref, t_ref, sems = refs
    base = HALF if which == 0 else 0
    copies = [
        pltpu.make_async_copy(down_hbm, kv_ref.at[pl.ds(0, HALF)], sems.at[0]),
        pltpu.make_async_copy(up_hbm, kv_ref.at[pl.ds(HALF, HALF)], sems.at[1]),
        pltpu.make_async_copy(q_hbm, q_ref, sems.at[2]),
        pltpu.make_async_copy(acc_hbm.at[pl.ds(base, HALF)], acc_ref, sems.at[3]),
        pltpu.make_async_copy(m_hbm.at[pl.ds(base, HALF)], m_ref, sems.at[4]),
        pltpu.make_async_copy(l_hbm.at[pl.ds(base, HALF)], l_ref, sems.at[5]),
    ]
    for copy in copies:
        copy.start()
    for copy in copies:
        copy.wait()
    run_list(kv_ref, q_ref, s_ref, t_ref, acc_ref, m_ref, l_ref, list_ref, n_ref[1 + which])
    if which == 0:

        def finish(n, carry):
            rows = []
            for h in range(2):
                out_ref[n, 128 * h : 128 * h + 128] = acc_ref[n, h].astype(jnp.bfloat16)
                rows += [m_ref[n, h, 0:1], jnp.sum(l_ref[n, h], axis=0, keepdims=True)]
            out_ref[n, 256:272] = stat_rows(rows)
            return carry

        lax.fori_loop(0, HALF, finish, 0)


def merge_kernel(acc_ref, m_ref, l_ref, got_ref, out_ref):
    def one(n, carry):
        stats = stats_of(got_ref[n, 256:272], 4)
        for h in range(2):
            mine, ours = m_ref[n, h, 0:1], jnp.sum(l_ref[n, h], axis=0, keepdims=True)
            his, theirs = stats[2 * h], stats[2 * h + 1]
            top = jnp.maximum(mine, his)
            a, b = jnp.exp2((mine - top) * LOG2), jnp.exp2((his - top) * LOG2)
            total = ours * a + theirs * b
            acc = acc_ref[n, h] * a + got_ref[n, 128 * h : 128 * h + 128].astype(jnp.float32) * b
            if h == 0:
                out_ref[n, 0:128] = (acc / total).astype(jnp.bfloat16)
            else:
                out_ref[n, 128:256] = acc.astype(jnp.bfloat16)
                out_ref[n, 256:272] = stat_rows([top, total])
        return carry

    lax.fori_loop(0, HALF, one, 0)


def final_kernel(got_ref, out_ref):
    for x in range(4):
        for pair in range(2):
            first, second = 4 * (2 * pair) + x, 4 * (2 * pair + 1) + x
            col = (6 * x + 3 * pair) * DH
            out_ref[:, col : col + DH] = got_ref[first, 0:128].T
            out_ref[:, col + DH : col + 2 * DH] = got_ref[second, 0:128].T
            m1, l1 = stats_of(got_ref[first, 256:272], 2)
            m2, l2 = stats_of(got_ref[second, 256:272], 2)
            top = jnp.maximum(m1, m2)
            a, b = jnp.exp2((m1 - top) * LOG2), jnp.exp2((m2 - top) * LOG2)
            total = l1 * a + l2 * b
            acc = got_ref[first, 128:256].astype(jnp.float32) * a
            acc = (acc + got_ref[second, 128:256].astype(jnp.float32) * b) / total
            out_ref[:, col + 2 * DH : col + 3 * DH] = acc.astype(jnp.bfloat16).T


def ring(x, axis):
    routes = [[(i, (i + far) % 4) for i in range(4)] for far in (1, 2, 3)]
    return [x] + [lax.ppermute(x, axis, route) for route in routes]


def shape(dims, dtype=jnp.bfloat16):
    return jax.ShapeDtypeStruct(dims, dtype)


def state(n):
    return [shape((n, 2, 128, 128), jnp.float32)] + [shape((n, 2, 8, 128), jnp.float32)] * 2


def run_lists(place, block_mask):
    return pl.pallas_call(
        lists_kernel,
        out_shape=[shape((n,), jnp.int32) for n in (FIRST_LEN, REST_LEN, HALO_LEN, HALO_LEN, 4)],
        in_specs=[SM, SM],
        out_specs=[SM] * 5,
        compiler_params=PARAMS,
        cost_estimate=pl.CostEstimate(flops=8 * 10**9, bytes_accessed=10**5, transcendentals=0),
        name="lists",
    )(place, block_mask)


def run_own(first, rest, counts, live, kv, text_rec, q, q_other):
    return pl.pallas_call(
        own_kernel,
        out_shape=state(SLAB),
        in_specs=[SM] * 4 + [ANY] * 4,
        out_specs=[VM] * 3,
        scratch_shapes=[
            pltpu.VMEM((HALF + 1, REC, DH), jnp.bfloat16),
            pltpu.VMEM((SLAB, QREC, DH), jnp.bfloat16),
            pltpu.VMEM((2, 768, DH), jnp.float32),
            pltpu.VMEM((2, 2, 8, DH), jnp.float32),
            pltpu.SemaphoreType.DMA((4,)),
        ],
        compiler_params=PARAMS,
        cost_estimate=pl.CostEstimate(flops=10**8, bytes_accessed=10**6, transcendentals=0),
        name="own_keys",
    )(first, rest, counts, live, kv, text_rec, q, q_other)


def run_text(live, kv, text_rec, tq):
    scratch = [pltpu.VMEM((1, 768, DH), jnp.float32), pltpu.VMEM((1, 2, 8, DH), jnp.float32)]
    return pl.pallas_call(
        text_kernel,
        out_shape=shape((2 * NTQ, 144, DH)),
        in_specs=[SM] + [VM] * 3,
        out_specs=VM,
        scratch_shapes=scratch + [pltpu.VMEM(s.shape, jnp.float32) for s in state(NTQ)],
        compiler_params=PARAMS,
        cost_estimate=pl.CostEstimate(flops=10**7, bytes_accessed=10**5, transcendentals=0),
        name="text_keys",
    )(live, kv, text_rec, tq)


def run_halo(which, queries, table, counts, from_down, from_up, acc, m, l):
    scratch = [
        pltpu.VMEM((SLAB, REC, DH), jnp.bfloat16),
        pltpu.VMEM((HALF, QREC, DH), jnp.bfloat16),
        pltpu.VMEM((2, 768, DH), jnp.float32),
            pltpu.VMEM((2, 2, 8, DH), jnp.float32),
    ]
    if which == 0:
        out = shape((HALF, OREC, DH))
        scratch += [pltpu.VMEM(s.shape, jnp.float32) for s in state(HALF)]
    else:
        out = state(HALF)
    return pl.pallas_call(
        functools.partial(halo_kernel, which),
        out_shape=out,
        in_specs=[SM, SM] + [ANY] * 6,
        out_specs=VM if which == 0 else [VM] * 3,
        scratch_shapes=scratch + [pltpu.SemaphoreType.DMA((6,))],
        compiler_params=PARAMS,
        cost_estimate=pl.CostEstimate(flops=2 * 10**9, bytes_accessed=10**7, transcendentals=4 * 10**6),
        name="halo_keys",
    )(table, counts, from_down, from_up, queries, acc, m, l)


def local(video_q, video_k, video_v, text_q, text_k, text_v, block_mask, text_count):
    f32 = jnp.float32
    together = lax.optimization_barrier
    y, z, c = lax.axis_index("y"), lax.axis_index("z"), lax.axis_index("c")
    pair, member = z // 2, z % 2
    chips = ("z", "x")
    swap = [(0, 1), (1, 0)]

    kv_send = pl.pallas_call(
        prep_kv_kernel, out_shape=shape((16, REC, DH)), in_specs=[ANY] * 2, out_specs=VM,
        scratch_shapes=[pltpu.VMEM((BLOCK, 24 * DH), jnp.bfloat16)] * 2 + [pltpu.SemaphoreType.DMA((6,))],
        compiler_params=pltpu.CompilerParams(vmem_limit_bytes=60 << 20), name="prep_kv",
    )(video_k, video_v)
    kv = lax.all_to_all(kv_send, chips, 0, 0, tiled=True)

    text_q, text_k, text_v, block_mask, _ = together((text_q, text_k, text_v, block_mask, kv_send))
    text = jnp.stack([text_q, text_k, text_v])
    text = jnp.where(c == pair, text, lax.ppermute(text, "c", swap))
    head = lax.dynamic_slice_in_dim(text, member * DH, DH, 2)
    shared = text[:, :, 2 * DH :]
    tq = jnp.stack([head[0].T, shared[0].T])
    tq = tq.reshape(2, DH, NTQ, DH).transpose(2, 0, 1, 3).reshape(NTQ, QREC, DH)
    mine = lax.dynamic_slice_in_dim(head, c * BLOCK, BLOCK, 1)
    half = lax.dynamic_slice_in_dim(shared, c * BLOCK + member * 64, 64, 1)
    vt = half[2].T
    text_rec = jnp.concatenate(
        [mine[1], half[1], mine[2].T, jnp.concatenate([vt[:64], vt[64:]], axis=1)], axis=0
    )[None]
    live_a = jnp.clip(text_count[0] - c * BLOCK, 0, BLOCK)
    live_c = jnp.clip(text_count[0] - c * BLOCK - member * 64, 0, 64)
    lead = y == 0
    live = jnp.stack([live_a, live_c, jnp.where(lead, live_a, 0), jnp.where(lead, live_c, 0)])
    live = live.astype(jnp.int32)
    place = jnp.stack([y, c]).astype(jnp.int32)
    first, rest, halo_a, halo_b, counts = run_lists(place, block_mask)
    video_q, tq, text_rec, first, rest, halo_a, halo_b, counts = together(
        (video_q, tq, text_rec, first, rest, halo_a, halo_b, counts)
    )
    q_send = pl.pallas_call(
        prep_q_kernel, out_shape=shape((16, QREC, DH)), in_specs=[VM], out_specs=VM,
        compiler_params=PARAMS, name="prep_q",
    )(video_q)

    q_send, kv = together((q_send, kv))
    from_down = lax.ppermute(kv, "y", [(0, 1), (1, 2), (2, 3)])
    from_up = lax.ppermute(kv, "y", [(1, 0), (2, 1), (3, 2)])
    q = lax.all_to_all(q_send, chips, 0, 0, tiled=True)
    text_part = run_text(live, kv, text_rec, tq)
    q, text_part = together((q, text_part))
    q_other = lax.ppermute(q, "c", swap)
    text_ring = ring(text_part, "z")
    acc, m, l = run_own(first, rest, counts, live, kv, text_rec, q, q_other)
    acc, *text_ring = together((acc, *text_ring))
    parts = jnp.stack(text_ring)[(z - jnp.arange(4)) % 4]
    theirs = lax.ppermute(lax.dynamic_slice_in_dim(parts, 2 - 2 * c, 2, 0), "c", swap)
    heads = pl.pallas_call(
        merge_text_kernel, out_shape=shape((3 * NTQ, 144, DH)), in_specs=[VM, VM], out_specs=VM,
        compiler_params=PARAMS, name="merge_text",
    )(lax.dynamic_slice_in_dim(parts, 2 * c, 2, 0), theirs)

    partial = run_halo(0, q_other, halo_a, counts, from_down, from_up, acc, m, l)
    q, heads = together((q, heads))
    got = lax.ppermute(partial, "c", swap)
    acc2, m2, l2 = run_halo(1, q, halo_b, counts, from_down, from_up, acc, m, l)
    record = pl.pallas_call(
        merge_kernel, out_shape=shape((HALF, OREC, DH)), in_specs=[VM] * 4, out_specs=VM,
        compiler_params=PARAMS, name="merge_cores",
    )(acc2, m2, l2, got)
    back = lax.all_to_all(record, chips, 0, 0, tiled=True)
    heads, _ = together((heads, record))
    text_out = pl.pallas_call(
        final_text_kernel, out_shape=shape((TEXT, 3 * DH)), in_specs=[VM] * 4, out_specs=VM,
        compiler_params=PARAMS, name="final_text",
    )(*ring(heads, "y"))
    video_out = pl.pallas_call(
        final_kernel, out_shape=shape((BLOCK, 24 * DH)), in_specs=[VM], out_specs=VM,
        compiler_params=PARAMS, name="final",
    )(back)
    return video_out, text_out


def solution(mesh):
    grid = Mesh(mesh.devices.reshape(4, 4, 4, 2), ("y", "z", "x", "c"))
    video = P(("y", "z", "x", "c"), None)
    text = P(None, ("x", "c"))
    return jax.shard_map(
        local,
        mesh=grid,
        in_specs=(video, video, video, text, text, text, P(), P()),
        out_specs=(video, text),
        check_vma=False,
    )
```

```python
import functools

import jax
import jax.numpy as jnp
import numpy as np
from jax import lax
from jax.experimental import pallas as pl
from jax.experimental.pallas import tpu as pltpu
from jax.sharding import Mesh, PartitionSpec as P

DH = 128
TEXT = 256
BLOCK = 128
SLAB = 32
HALF = 16
NTQ = 2
REC = 384
QREC = 256
OREC = 272
STEP = 4
UNROLL = 4
LOG2 = float(DH**-0.5 * np.log2(np.e))
neg_fill = -1e30
FLAG = 4096
FIRST_LEN = SLAB * STEP
PAD = (UNROLL + 2) * STEP
REST_LEN = SLAB * (HALF + STEP) + PAD
HALO_LEN = HALF * (2 * HALF + STEP) + PAD

VM = pl.BlockSpec(memory_space=pltpu.VMEM)
SM = pl.BlockSpec(memory_space=pltpu.SMEM)
ANY = pl.BlockSpec(memory_space=pl.ANY)
PARAMS = pltpu.CompilerParams(vmem_limit_bytes=20 << 20)


def head_a(chip):
    z, x = chip // 4, chip % 4
    return 6 * x + 3 * (z // 2) + z % 2


def head_c(chip):
    z, x = chip // 4, chip % 4
    return 6 * x + 3 * (z // 2) + 2


def packed(vt, half):
    cols = vt[:, 64 * half : 64 * half + 64]
    return jnp.concatenate([cols[:64], cols[64:]], axis=1)


def prep_kv_kernel(k_hbm, v_hbm, out_ref, k_ref, v_ref, sems):
    third = 8 * DH
    copies = [
        [
            pltpu.make_async_copy(
                hbm.at[:, pl.ds(third * i, third)], ref.at[:, pl.ds(third * i, third)], sems.at[2 * i + j]
            )
            for j, (hbm, ref) in enumerate(((k_hbm, k_ref), (v_hbm, v_ref)))
        ]
        for i in range(3)
    ]
    for pair in copies:
        for copy in pair:
            copy.start()
    arrived = 0
    for x in range(4):
        while 8 * arrived < 6 * (x + 1):
            for copy in copies[arrived]:
                copy.wait()
            arrived += 1
        for z in range(4):
            chip = 4 * z + x
            a, c, half = head_a(chip) * DH, head_c(chip) * DH, z % 2
            out_ref[chip, 0:128] = k_ref[:, a : a + DH]
            out_ref[chip, 128:192] = k_ref[64 * half : 64 * half + 64, c : c + DH]
            out_ref[chip, 192:320] = v_ref[:, a : a + DH].T
            out_ref[chip, 320:384] = packed(v_ref[:, c : c + DH].T, half)


def prep_q_kernel(q_ref, out_ref):
    for chip in range(16):
        a, c = head_a(chip) * DH, head_c(chip) * DH
        out_ref[chip, 0:128] = q_ref[:, a : a + DH].T
        out_ref[chip, 128:256] = q_ref[:, c : c + DH].T


def lists_kernel(place_ref, mask_ref, first_ref, rest_ref, halo_a_ref, halo_b_ref, n_ref):
    y, c = place_ref[0], place_ref[1]

    def kept(q, j, dy):
        col = (y + dy) * SLAB + 2 * j + c
        inside = jnp.logical_and(col >= 0, col < 4 * SLAB)
        value = mask_ref[y * SLAB + q, jnp.clip(col, 0, 4 * SLAB - 1)]
        return jnp.where(inside, value, 0)

    def row_of(n):
        return jnp.where(n < HALF, 2 * n + c, 2 * (n - HALF) + 1 - c)

    def close(ref, start, pos, size):
        last = ref[jnp.maximum(pos - 1, 0)]
        for _ in range(size - 1):
            missing = (pos - start) % size != 0

            @pl.when(missing)
            def _():
                ref[pos] = last | FLAG

            pos = pos + jnp.where(missing, 1, 0)
        return pos

    def own(n, pos):
        row = row_of(n)
        count = jnp.int32(0)
        start = pos
        for j in range(HALF):
            hit = kept(row, j, 0)

            @pl.when(jnp.logical_and(hit > 0, count < STEP - 1))
            def _():
                first_ref[n * STEP + count] = n * 64 + j

            @pl.when(jnp.logical_and(hit > 0, count >= STEP - 1))
            def _():
                rest_ref[pos] = n * 64 + j

            pos = pos + jnp.where(jnp.logical_and(hit > 0, count >= STEP - 1), 1, 0)
            count = count + hit
        some = jnp.minimum(count, STEP - 1)
        last = jnp.where(some > 0, first_ref[n * STEP + jnp.maximum(some - 1, 0)], n * 64)
        for k in range(STEP):

            @pl.when(k >= some)
            def _():
                first_ref[n * STEP + k] = last | FLAG

        return close(rest_ref, start, pos, STEP)

    end = lax.fori_loop(0, SLAB, own, jnp.int32(0))
    n_ref[0] = end // STEP
    for k in range(PAD):
        rest_ref[end + k] = FLAG | SLAB * 64
    for which, (ref, base) in enumerate(((halo_a_ref, HALF), (halo_b_ref, 0))):

        def far(n, pos):
            start = pos
            row = row_of(n + base)
            for dy, shift in ((-1, 0), (1, HALF)):
                for j in range(HALF):
                    hit = kept(row, j, dy)

                    @pl.when(hit > 0)
                    def _():
                        ref[pos] = n * 64 + shift + j

                    pos = pos + hit
            return close(ref, start, pos, STEP)

        end = lax.fori_loop(0, HALF, far, jnp.int32(0))
        n_ref[1 + which] = end // STEP
        for k in range(PAD):
            ref[end + k] = FLAG | HALF * 64
    n_ref[3] = 0


def fold(x, op):
    return op(x.reshape(-1, 8, DH), axis=0)


def slots(list_ref, t):
    codes = [list_ref[STEP * t + k] for k in range(STEP)]
    q = (codes[0] & (FLAG - 1)) >> 6
    gaps = [jnp.where(code >= FLAG, jnp.float32(1e30), jnp.float32(0)) for code in codes]
    return q, [code & 63 for code in codes], gaps


def wide_c(kv_ref, js):
    low, high = [], []
    for j in js:
        part = kv_ref[j, 320:384]
        low.append(part[:, :64])
        high.append(part[:, 64:])
    return jnp.concatenate([jnp.concatenate(low, axis=1), jnp.concatenate(high, axis=1)], axis=0)


class Work:
    def __init__(self, kv, q, s, p, top, factor, acc, m, l):
        self.kv, self.q, self.s, self.p, self.top, self.factor = kv, q, s, p, top, factor
        self.acc, self.m, self.l = acc, m, l


def scores(work, buf, q, js, live=None):
    for h, (low, size, row) in enumerate(((0, 128, 0), (512, 64, 128))):
        keys = jnp.concatenate([work.kv[j, row : row + size] for j in js], axis=0)
        s = jnp.dot(keys, work.q[q, 128 * h : 128 * h + 128], preferred_element_type=jnp.float32)
        if live is not None:
            rows = lax.broadcasted_iota(jnp.int32, (size, DH), 0)
            s = jnp.concatenate([jnp.where(rows < live[h], s[:size], neg_fill), s[size:]], axis=0)
        work.s[buf, low : low + STEP * size] = s
        work.top[buf, h] = jnp.broadcast_to(column_max(s), (8, DH))


def column_max(s):
    return jnp.max(fold(s, jnp.max), axis=0, keepdims=True)


def values_of(kv_ref, js, h):
    if h == 0:
        return jnp.concatenate([kv_ref[j, 192:320] for j in js], axis=1)
    return wide_c(kv_ref, js)


def soften(work, buf, q, gaps, first=False):
    for h in range(2):
        top = work.top[buf, h]
        if not first:
            old = work.m[q, h]
            top = jnp.maximum(old, top)
            factor = jnp.exp2((old - top) * LOG2)
            work.factor[buf, h] = factor
        low, size = (0, 128) if h == 0 else (512, 64)
        sums = []
        for k, gap in enumerate(gaps):
            rows = slice(low + size * k, low + size * (k + 1))
            w = jnp.exp2((work.s[buf, rows] - (top[:1] + gap)) * LOG2)
            sums.append(fold(w, jnp.sum))
            work.p[buf, rows] = w.astype(jnp.bfloat16)
        total = sum(sums)
        work.m[q, h] = top
        work.l[q, h] = total if first else work.l[q, h] * factor + total


def gather(work, buf, q, js, first=False):
    for h, rows in enumerate((slice(0, 512), slice(512, 768))):
        out = jnp.dot(values_of(work.kv, js, h), work.p[buf, rows], preferred_element_type=jnp.float32)
        work.acc[q, h] = out if first else work.acc[q, h] * work.factor[buf, h, 0:1] + out


def pipelined(score, soft, add, rounds):
    score(0, 0)
    score(1, 1)
    soft(0, 0)

    def body(i, carry):
        for k in range(UNROLL):
            t = UNROLL * i + k
            score(t + 2, k % 2)
            add(t, k % 2)
            soft(t + 1, (k + 1) % 2)
        return carry

    lax.fori_loop(0, rounds, body, 0)


def run_list(work, list_ref, steps):
    def score(t, buf):
        q, js, _ = slots(list_ref, t)
        scores(work, buf, q, js)

    def soft(t, buf):
        q, _, gaps = slots(list_ref, t)
        soften(work, buf, q, gaps)

    def add(t, buf):
        q, js, _ = slots(list_ref, t)
        gather(work, buf, q, js)

    pipelined(score, soft, add, (steps + UNROLL - 1) // UNROLL)


def own_kernel(
    first_ref, rest_ref, n_ref, live_ref, kv_hbm, text_hbm, q_hbm, other_hbm,
    acc_ref, m_ref, l_ref, kv_ref, q_ref, s_ref, p_ref, t_ref, f_ref, sems,
):
    copies = [
        pltpu.make_async_copy(kv_hbm, kv_ref.at[pl.ds(0, HALF)], sems.at[0]),
        pltpu.make_async_copy(text_hbm, kv_ref.at[pl.ds(HALF, 1)], sems.at[1]),
        pltpu.make_async_copy(q_hbm, q_ref.at[pl.ds(0, HALF)], sems.at[2]),
        pltpu.make_async_copy(other_hbm, q_ref.at[pl.ds(HALF, HALF)], sems.at[3]),
    ]
    work = Work(kv_ref, q_ref, s_ref, p_ref, t_ref, f_ref, acc_ref, m_ref, l_ref)
    for copy in copies:
        copy.start()
    for copy in copies:
        copy.wait()

    def line(n):
        codes = [first_ref[STEP * n + k] for k in range(STEP - 1)]
        gaps = [jnp.float32(0)]
        gaps += [jnp.where(code >= FLAG, jnp.float32(1e30), jnp.float32(0)) for code in codes]
        return [jnp.int32(HALF)] + [code & 63 for code in codes], gaps

    def score(n, buf):
        n = jnp.minimum(n, SLAB - 1)
        scores(work, buf, n, line(n)[0], (live_ref[0], live_ref[1]))

    def soft(n, buf):
        n = jnp.minimum(n, SLAB - 1)
        soften(work, buf, n, line(n)[1], True)

    def add(n, buf):
        gather(work, buf, n, line(n)[0], True)

    pipelined(score, soft, add, SLAB // UNROLL)
    run_list(work, rest_ref, n_ref[0])


def text_kernel(
    live_ref, kv_ref, text_ref, q_ref, out_ref, s_ref, p_ref, t_ref, f_ref, acc_ref, m_ref, l_ref
):
    none = [jnp.float32(0)] * STEP
    live = (live_ref[2], live_ref[3])
    work = Work(kv_ref, q_ref, s_ref, p_ref, t_ref, f_ref, acc_ref, m_ref, l_ref)

    for start in range(0, HALF, STEP):
        js = list(range(start, start + STEP))
        for block in range(NTQ):
            scores(work, block, block, js)
        for block in range(NTQ):
            soften(work, block, block, none, start == 0)
        for block in range(NTQ):
            gather(work, block, block, js, start == 0)
    for block in range(NTQ):
        for h, (low, size, row) in enumerate(((0, 128, 0), (512, 64, 128))):
            s = jnp.dot(
                text_ref[0, row : row + size],
                q_ref[block, 128 * h : 128 * h + 128],
                preferred_element_type=jnp.float32,
            )
            rows = lax.broadcasted_iota(jnp.int32, s.shape, 0)
            s = jnp.where(rows < live[h], s, neg_fill)
            old = m_ref[block, h]
            new = jnp.maximum(old, column_max(s))
            factor = jnp.exp2((old - new) * LOG2)
            w = jnp.exp2((s - new[:1]) * LOG2)
            total = row_sum(l_ref[block, h] * factor) + row_sum(fold(w, jnp.sum))
            v = text_ref[0, 192:320] if h == 0 else wide_c(text_ref, [0])
            acc = acc_ref[block, h] * factor[:1] + jnp.dot(
                v, w.astype(jnp.bfloat16), preferred_element_type=jnp.float32
            )
            put_text(out_ref, h * NTQ + block, new[:1], total, acc)


def row_sum(x):
    return jnp.sum(x, axis=0, keepdims=True)


def put_text(ref, at, top, total, acc):
    ref[at, 0:128] = acc.astype(jnp.bfloat16)
    ref[at, 128:144] = stat_rows([top, total])


def merged(blocks):
    stats = [stats_of(block[128:144], 2) for block in blocks]
    top = functools.reduce(jnp.maximum, [s[0] for s in stats])
    factors = [jnp.exp2((s[0] - top) * LOG2) for s in stats]
    total = sum(s[1] * f for s, f in zip(stats, factors))
    return top, total, sum(b[0:128].astype(jnp.float32) * f for b, f in zip(blocks, factors))


def merge_text_kernel(member_ref, here_ref, there_ref, out_ref):
    first = member_ref[0] == 0
    rows = 2 * NTQ
    for block in range(NTQ):
        for head in range(3):
            at = (0 if head < 2 else NTQ) + block
            pairs = [(here_ref[core * rows + at], there_ref[core * rows + at]) for core in range(2)]
            if head == 2:
                blocks = [part for both in pairs for part in both]
            else:
                ours = first if head == 0 else jnp.logical_not(first)
                blocks = [jnp.where(ours, *both) for both in pairs]
            put_text(out_ref, head * NTQ + block, *merged(blocks))


def final_text_kernel(*refs):
    for block in range(NTQ):
        for head in range(3):
            _, total, acc = merged([ref[head * NTQ + block] for ref in refs[:-1]])
            out = (acc / total).astype(jnp.bfloat16).T
            refs[-1][128 * block : 128 * block + 128, head * DH : head * DH + DH] = out


def split3(x):
    rows = []
    for _ in range(3):
        part = x.astype(jnp.bfloat16)
        rows.append(part)
        x = x - part.astype(jnp.float32)
    return rows


def stat_rows(rows):
    parts = [part for row in rows for part in split3(row)]
    pad = jnp.zeros((16 - len(parts), DH), jnp.bfloat16)
    return jnp.concatenate(parts + [pad], axis=0)


def stats_of(block, count):
    x = block.astype(jnp.float32)
    return [x[3 * i : 3 * i + 1] + x[3 * i + 1 : 3 * i + 2] + x[3 * i + 2 : 3 * i + 3] for i in range(count)]


def halo_kernel(
    which, list_ref, n_ref, down_hbm, up_hbm, q_hbm, acc_hbm, m_hbm, l_hbm,
    *refs,
):
    if which == 0:
        out_ref, kv_ref, q_ref, s_ref, p_ref, t_ref, f_ref, acc_ref, m_ref, l_ref, sems = refs
    else:
        acc_ref, m_ref, l_ref, kv_ref, q_ref, s_ref, p_ref, t_ref, f_ref, sems = refs
    base = HALF if which == 0 else 0
    copies = [
        pltpu.make_async_copy(down_hbm, kv_ref.at[pl.ds(0, HALF)], sems.at[0]),
        pltpu.make_async_copy(up_hbm, kv_ref.at[pl.ds(HALF, HALF)], sems.at[1]),
        pltpu.make_async_copy(q_hbm, q_ref.at[pl.ds(0, HALF)], sems.at[2]),
        pltpu.make_async_copy(acc_hbm.at[pl.ds(base, HALF)], acc_ref.at[pl.ds(0, HALF)], sems.at[3]),
        pltpu.make_async_copy(m_hbm.at[pl.ds(base, HALF)], m_ref.at[pl.ds(0, HALF)], sems.at[4]),
        pltpu.make_async_copy(l_hbm.at[pl.ds(base, HALF)], l_ref.at[pl.ds(0, HALF)], sems.at[5]),
    ]
    for copy in copies:
        copy.start()
    for copy in copies:
        copy.wait()
    work = Work(kv_ref, q_ref, s_ref, p_ref, t_ref, f_ref, acc_ref, m_ref, l_ref)
    run_list(work, list_ref, n_ref[1 + which])
    if which == 0:

        def finish(n, carry):
            rows = []
            for h in range(2):
                out_ref[n, 128 * h : 128 * h + 128] = acc_ref[n, h].astype(jnp.bfloat16)
                rows += [m_ref[n, h, 0:1], jnp.sum(l_ref[n, h], axis=0, keepdims=True)]
            out_ref[n, 256:272] = stat_rows(rows)
            return carry

        lax.fori_loop(0, HALF, finish, 0)


def merge_kernel(acc_ref, m_ref, l_ref, got_ref, out_ref):
    def one(n, carry):
        stats = stats_of(got_ref[n, 256:272], 4)
        for h in range(2):
            mine, ours = m_ref[n, h, 0:1], jnp.sum(l_ref[n, h], axis=0, keepdims=True)
            his, theirs = stats[2 * h], stats[2 * h + 1]
            top = jnp.maximum(mine, his)
            a, b = jnp.exp2((mine - top) * LOG2), jnp.exp2((his - top) * LOG2)
            total = ours * a + theirs * b
            acc = acc_ref[n, h] * a + got_ref[n, 128 * h : 128 * h + 128].astype(jnp.float32) * b
            if h == 0:
                out_ref[n, 0:128] = (acc / total).astype(jnp.bfloat16)
            else:
                out_ref[n, 128:256] = acc.astype(jnp.bfloat16)
                out_ref[n, 256:272] = stat_rows([top, total])
        return carry

    lax.fori_loop(0, HALF, one, 0)


def final_kernel(got_ref, out_ref):
    for x in range(4):
        for pair in range(2):
            first, second = 4 * (2 * pair) + x, 4 * (2 * pair + 1) + x
            col = (6 * x + 3 * pair) * DH
            out_ref[:, col : col + DH] = got_ref[first, 0:128].T
            out_ref[:, col + DH : col + 2 * DH] = got_ref[second, 0:128].T
            m1, l1 = stats_of(got_ref[first, 256:272], 2)
            m2, l2 = stats_of(got_ref[second, 256:272], 2)
            top = jnp.maximum(m1, m2)
            a, b = jnp.exp2((m1 - top) * LOG2), jnp.exp2((m2 - top) * LOG2)
            total = l1 * a + l2 * b
            acc = got_ref[first, 128:256].astype(jnp.float32) * a
            acc = (acc + got_ref[second, 128:256].astype(jnp.float32) * b) / total
            out_ref[:, col + 2 * DH : col + 3 * DH] = acc.astype(jnp.bfloat16).T


def ring(x, axis):
    routes = [[(i, (i + far) % 4) for i in range(4)] for far in (1, 2, 3)]
    return [x] + [lax.ppermute(x, axis, route) for route in routes]


def shape(dims, dtype=jnp.bfloat16):
    return jax.ShapeDtypeStruct(dims, dtype)


def state(n):
    return [shape((n, 2, 128, 128), jnp.float32)] + [shape((n, 2, 8, 128), jnp.float32)] * 2


def run_lists(place, block_mask):
    return pl.pallas_call(
        lists_kernel,
        out_shape=[shape((n,), jnp.int32) for n in (FIRST_LEN, REST_LEN, HALO_LEN, HALO_LEN, 4)],
        in_specs=[SM, SM],
        out_specs=[SM] * 5,
        compiler_params=PARAMS,
        cost_estimate=pl.CostEstimate(flops=8 * 10**9, bytes_accessed=10**5, transcendentals=0),
        name="lists",
    )(place, block_mask)


def run_own(first, rest, counts, live, kv, text_rec, q, q_other):
    return pl.pallas_call(
        own_kernel,
        out_shape=state(SLAB + 1),
        in_specs=[SM] * 4 + [ANY] * 4,
        out_specs=[VM] * 3,
        scratch_shapes=[
            pltpu.VMEM((HALF + 1, REC, DH), jnp.bfloat16),
            pltpu.VMEM((SLAB + 1, QREC, DH), jnp.bfloat16),
            pltpu.VMEM((2, 768, DH), jnp.float32),
            pltpu.VMEM((2, 768, DH), jnp.bfloat16),
            pltpu.VMEM((2, 2, 8, DH), jnp.float32),
            pltpu.VMEM((2, 2, 8, DH), jnp.float32),
            pltpu.SemaphoreType.DMA((4,)),
        ],
        compiler_params=PARAMS,
        cost_estimate=pl.CostEstimate(flops=10**8, bytes_accessed=10**6, transcendentals=0),
        name="own_keys",
    )(first, rest, counts, live, kv, text_rec, q, q_other)


def run_text(live, kv, text_rec, tq):
    scratch = [pltpu.VMEM((NTQ, 768, DH), jnp.float32), pltpu.VMEM((NTQ, 768, DH), jnp.bfloat16)]
    scratch += [pltpu.VMEM((NTQ, 2, 8, DH), jnp.float32)] * 2
    return pl.pallas_call(
        text_kernel,
        out_shape=shape((2 * NTQ, 144, DH)),
        in_specs=[SM] + [VM] * 3,
        out_specs=VM,
        scratch_shapes=scratch + [pltpu.VMEM(s.shape, jnp.float32) for s in state(NTQ)],
        compiler_params=PARAMS,
        cost_estimate=pl.CostEstimate(flops=10**7, bytes_accessed=10**5, transcendentals=0),
        name="text_keys",
    )(live, kv, text_rec, tq)


def run_halo(which, queries, table, counts, from_down, from_up, acc, m, l):
    scratch = [
        pltpu.VMEM((SLAB, REC, DH), jnp.bfloat16),
        pltpu.VMEM((HALF + 1, QREC, DH), jnp.bfloat16),
        pltpu.VMEM((2, 768, DH), jnp.float32),
        pltpu.VMEM((2, 768, DH), jnp.bfloat16),
        pltpu.VMEM((2, 2, 8, DH), jnp.float32),
        pltpu.VMEM((2, 2, 8, DH), jnp.float32),
    ]
    if which == 0:
        out = shape((HALF, OREC, DH))
        scratch += [pltpu.VMEM(s.shape, jnp.float32) for s in state(HALF + 1)]
    else:
        out = state(HALF + 1)
    return pl.pallas_call(
        functools.partial(halo_kernel, which),
        out_shape=out,
        in_specs=[SM, SM] + [ANY] * 6,
        out_specs=VM if which == 0 else [VM] * 3,
        scratch_shapes=scratch + [pltpu.SemaphoreType.DMA((6,))],
        compiler_params=PARAMS,
        cost_estimate=pl.CostEstimate(flops=2 * 10**9, bytes_accessed=10**7, transcendentals=4 * 10**6),
        name="halo_keys",
    )(table, counts, from_down, from_up, queries, acc, m, l)


def local(video_q, video_k, video_v, text_q, text_k, text_v, block_mask, text_count):
    f32 = jnp.float32
    together = lax.optimization_barrier
    y, z, c = lax.axis_index("y"), lax.axis_index("z"), lax.axis_index("c")
    pair, member = z // 2, z % 2
    chips = ("z", "x")
    swap = [(0, 1), (1, 0)]

    kv_send = pl.pallas_call(
        prep_kv_kernel, out_shape=shape((16, REC, DH)), in_specs=[ANY] * 2, out_specs=VM,
        scratch_shapes=[pltpu.VMEM((BLOCK, 24 * DH), jnp.bfloat16)] * 2 + [pltpu.SemaphoreType.DMA((6,))],
        compiler_params=pltpu.CompilerParams(vmem_limit_bytes=60 << 20), name="prep_kv",
    )(video_k, video_v)
    kv = lax.all_to_all(kv_send, chips, 0, 0, tiled=True)

    text_q, text_k, text_v, block_mask, _ = together((text_q, text_k, text_v, block_mask, kv_send))
    text = jnp.stack([text_q, text_k, text_v])
    text = jnp.where(c == pair, text, lax.ppermute(text, "c", swap))
    head = lax.dynamic_slice_in_dim(text, member * DH, DH, 2)
    shared = text[:, :, 2 * DH :]
    tq = jnp.stack([head[0].T, shared[0].T])
    tq = tq.reshape(2, DH, NTQ, DH).transpose(2, 0, 1, 3).reshape(NTQ, QREC, DH)
    mine = lax.dynamic_slice_in_dim(head, c * BLOCK, BLOCK, 1)
    half = lax.dynamic_slice_in_dim(shared, c * BLOCK + member * 64, 64, 1)
    vt = half[2].T
    text_rec = jnp.concatenate(
        [mine[1], half[1], mine[2].T, jnp.concatenate([vt[:64], vt[64:]], axis=1)], axis=0
    )[None]
    live_a = jnp.clip(text_count[0] - c * BLOCK, 0, BLOCK)
    live_c = jnp.clip(text_count[0] - c * BLOCK - member * 64, 0, 64)
    lead = y == 0
    live = jnp.stack([live_a, live_c, jnp.where(lead, live_a, 0), jnp.where(lead, live_c, 0)])
    live = live.astype(jnp.int32)
    place = jnp.stack([y, c]).astype(jnp.int32)
    first, rest, halo_a, halo_b, counts = run_lists(place, block_mask)
    video_q, tq, text_rec, first, rest, halo_a, halo_b, counts = together(
        (video_q, tq, text_rec, first, rest, halo_a, halo_b, counts)
    )
    q_send = pl.pallas_call(
        prep_q_kernel, out_shape=shape((16, QREC, DH)), in_specs=[VM], out_specs=VM,
        compiler_params=PARAMS, name="prep_q",
    )(video_q)

    q_send, kv = together((q_send, kv))
    from_down = lax.ppermute(kv, "y", [(0, 1), (1, 2), (2, 3)])
    from_up = lax.ppermute(kv, "y", [(1, 0), (2, 1), (3, 2)])
    q = lax.all_to_all(q_send, chips, 0, 0, tiled=True)
    text_part = run_text(live, kv, text_rec, tq)
    here = jnp.concatenate([text_part, lax.ppermute(text_part, "c", swap)])
    q, here = together((q, here))
    q_other = lax.ppermute(q, "c", swap)
    there = lax.ppermute(here, "z", [(0, 1), (1, 0), (2, 3), (3, 2)])
    acc, m, l = run_own(first, rest, counts, live, kv, text_rec, q, q_other)
    acc, there = together((acc, there))
    heads = pl.pallas_call(
        merge_text_kernel, out_shape=shape((3 * NTQ, 144, DH)), in_specs=[SM, VM, VM], out_specs=VM,
        compiler_params=PARAMS, name="merge_text",
    )(member.astype(jnp.int32)[None], here, there)
    acc, heads = together((acc, heads))
    far = lax.ppermute(heads, "z", [(0, 2), (1, 3), (2, 0), (3, 1)])
    heads = jnp.where(c == pair, heads, far)

    partial = run_halo(0, q_other, halo_a, counts, from_down, from_up, acc, m, l)
    got = lax.ppermute(partial, "c", swap)
    acc2, m2, l2 = run_halo(1, q, halo_b, counts, from_down, from_up, acc, m, l)
    got, heads = together((got, heads))
    record = pl.pallas_call(
        merge_kernel, out_shape=shape((HALF, OREC, DH)), in_specs=[VM] * 4, out_specs=VM,
        compiler_params=PARAMS, name="merge_cores",
    )(acc2, m2, l2, got)
    back = lax.all_to_all(record, chips, 0, 0, tiled=True)
    heads, _ = together((heads, record))
    text_out = pl.pallas_call(
        final_text_kernel, out_shape=shape((TEXT, 3 * DH)), in_specs=[VM] * 4, out_specs=VM,
        compiler_params=PARAMS, name="final_text",
    )(*ring(heads, "y"))
    video_out = pl.pallas_call(
        final_kernel, out_shape=shape((BLOCK, 24 * DH)), in_specs=[VM], out_specs=VM,
        compiler_params=PARAMS, name="final",
    )(back)
    return video_out, text_out


def solution(mesh):
    grid = Mesh(mesh.devices.reshape(4, 4, 4, 2), ("y", "z", "x", "c"))
    video = P(("y", "z", "x", "c"), None)
    text = P(None, ("x", "c"))
    return jax.shard_map(
        local,
        mesh=grid,
        in_specs=(video, video, video, text, text, text, P(), P()),
        out_specs=(video, text),
        check_vma=False,
    )
```

```python
import functools

import jax
import jax.numpy as jnp
import numpy as np
from jax import lax
from jax.experimental import pallas as pl
from jax.experimental.pallas import tpu as pltpu
from jax.sharding import Mesh, PartitionSpec as P

DH = 128
TEXT = 256
BLOCK = 128
SLAB = 32
HALF = 16
NTQ = 2
REC = 384
QREC = 256
OREC = 272
STEP = 4
UNROLL = 8
LOG2 = float(DH**-0.5 * np.log2(np.e))
neg_fill = -1e30
FLAG = 4096
FIRST_LEN = SLAB * STEP
PAD = (UNROLL + 2) * STEP
REST_LEN = SLAB * (HALF + STEP) + PAD
HALO_LEN = HALF * (2 * HALF + STEP) + PAD

VM = pl.BlockSpec(memory_space=pltpu.VMEM)
SM = pl.BlockSpec(memory_space=pltpu.SMEM)
ANY = pl.BlockSpec(memory_space=pl.ANY)
PARAMS = pltpu.CompilerParams(vmem_limit_bytes=20 << 20)


def head_a(chip):
    z, x = chip // 4, chip % 4
    return 6 * x + 3 * (z // 2) + z % 2


def head_c(chip):
    z, x = chip // 4, chip % 4
    return 6 * x + 3 * (z // 2) + 2


def packed(vt, half):
    cols = vt[:, 64 * half : 64 * half + 64]
    return jnp.concatenate([cols[:64], cols[64:]], axis=1)


def prep_kv_kernel(k_hbm, v_hbm, out_ref, k_ref, v_ref, sems):
    third = 8 * DH
    copies = [
        [
            pltpu.make_async_copy(
                hbm.at[:, pl.ds(third * i, third)], ref.at[:, pl.ds(third * i, third)], sems.at[2 * i + j]
            )
            for j, (hbm, ref) in enumerate(((k_hbm, k_ref), (v_hbm, v_ref)))
        ]
        for i in range(3)
    ]
    for pair in copies:
        for copy in pair:
            copy.start()
    arrived = 0
    for x in range(4):
        while 8 * arrived < 6 * (x + 1):
            for copy in copies[arrived]:
                copy.wait()
            arrived += 1
        for z in range(4):
            chip = 4 * z + x
            a, c, half = head_a(chip) * DH, head_c(chip) * DH, z % 2
            out_ref[chip, 0:128] = k_ref[:, a : a + DH]
            out_ref[chip, 128:192] = k_ref[64 * half : 64 * half + 64, c : c + DH]
            out_ref[chip, 192:320] = v_ref[:, a : a + DH].T
            out_ref[chip, 320:384] = packed(v_ref[:, c : c + DH].T, half)


def prep_q_kernel(q_ref, out_ref):
    for chip in range(16):
        a, c = head_a(chip) * DH, head_c(chip) * DH
        out_ref[chip, 0:128] = q_ref[:, a : a + DH].T
        out_ref[chip, 128:256] = q_ref[:, c : c + DH].T


def lists_kernel(place_ref, mask_ref, first_ref, rest_ref, halo_a_ref, halo_b_ref, n_ref):
    y, c = place_ref[0], place_ref[1]

    def kept(q, j, dy):
        col = (y + dy) * SLAB + 2 * j + c
        inside = jnp.logical_and(col >= 0, col < 4 * SLAB)
        value = mask_ref[y * SLAB + q, jnp.clip(col, 0, 4 * SLAB - 1)]
        return jnp.where(inside, value, 0)

    def row_of(n):
        return jnp.where(n < HALF, 2 * n + c, 2 * (n - HALF) + 1 - c)

    def close(ref, start, pos, size):
        last = ref[jnp.maximum(pos - 1, 0)]
        for _ in range(size - 1):
            missing = (pos - start) % size != 0

            @pl.when(missing)
            def _():
                ref[pos] = last | FLAG

            pos = pos + jnp.where(missing, 1, 0)
        return pos

    def own(n, pos):
        row = row_of(n)
        count = jnp.int32(0)
        start = pos
        for j in range(HALF):
            hit = kept(row, j, 0)

            @pl.when(jnp.logical_and(hit > 0, count < STEP - 1))
            def _():
                first_ref[n * STEP + count] = n * 64 + j

            @pl.when(jnp.logical_and(hit > 0, count >= STEP - 1))
            def _():
                rest_ref[pos] = n * 64 + j

            pos = pos + jnp.where(jnp.logical_and(hit > 0, count >= STEP - 1), 1, 0)
            count = count + hit
        some = jnp.minimum(count, STEP - 1)
        last = jnp.where(some > 0, first_ref[n * STEP + jnp.maximum(some - 1, 0)], n * 64)
        for k in range(STEP):

            @pl.when(k >= some)
            def _():
                first_ref[n * STEP + k] = last | FLAG

        return close(rest_ref, start, pos, STEP)

    end = lax.fori_loop(0, SLAB, own, jnp.int32(0))
    n_ref[0] = end // STEP
    for k in range(PAD):
        rest_ref[end + k] = FLAG | SLAB * 64
    for which, (ref, base) in enumerate(((halo_a_ref, HALF), (halo_b_ref, 0))):

        def far(n, pos):
            start = pos
            row = row_of(n + base)
            for dy, shift in ((-1, 0), (1, HALF)):
                for j in range(HALF):
                    hit = kept(row, j, dy)

                    @pl.when(hit > 0)
                    def _():
                        ref[pos] = n * 64 + shift + j

                    pos = pos + hit
            return close(ref, start, pos, STEP)

        end = lax.fori_loop(0, HALF, far, jnp.int32(0))
        n_ref[1 + which] = end // STEP
        for k in range(PAD):
            ref[end + k] = FLAG | HALF * 64
    n_ref[3] = 0


def fold(x, op):
    return op(x.reshape(-1, 8, DH), axis=0)


def slots(list_ref, t):
    codes = [list_ref[STEP * t + k] for k in range(STEP)]
    q = (codes[0] & (FLAG - 1)) >> 6
    gaps = [jnp.where(code >= FLAG, jnp.float32(1e30), jnp.float32(0)) for code in codes]
    return q, [code & 63 for code in codes], gaps


def wide_c(kv_ref, js):
    low, high = [], []
    for j in js:
        part = kv_ref[j, 320:384]
        low.append(part[:, :64])
        high.append(part[:, 64:])
    return jnp.concatenate([jnp.concatenate(low, axis=1), jnp.concatenate(high, axis=1)], axis=0)


class Work:
    def __init__(self, kv, q, s, p, top, factor, acc, m, l):
        self.kv, self.q, self.s, self.p, self.top, self.factor = kv, q, s, p, top, factor
        self.acc, self.m, self.l = acc, m, l


def scores(work, buf, q, js, live=None):
    for h, (low, size, row) in enumerate(((0, 128, 0), (512, 64, 128))):
        keys = jnp.concatenate([work.kv[j, row : row + size] for j in js], axis=0)
        s = jnp.dot(keys, work.q[q, 128 * h : 128 * h + 128], preferred_element_type=jnp.float32)
        if live is not None:
            rows = lax.broadcasted_iota(jnp.int32, (size, DH), 0)
            s = jnp.concatenate([jnp.where(rows < live[h], s[:size], neg_fill), s[size:]], axis=0)
        work.s[buf, low : low + STEP * size] = s
        work.top[buf, h] = jnp.broadcast_to(column_max(s), (8, DH))


def column_max(s):
    return jnp.max(fold(s, jnp.max), axis=0, keepdims=True)


def values_of(kv_ref, js, h):
    if h == 0:
        return jnp.concatenate([kv_ref[j, 192:320] for j in js], axis=1)
    return wide_c(kv_ref, js)


def soften(work, buf, q, gaps, first=False):
    for h in range(2):
        top = work.top[buf, h]
        if not first:
            old = work.m[q, h]
            top = jnp.maximum(old, top)
            factor = jnp.exp2((old - top) * LOG2)
            work.factor[buf, h] = factor
        low, size = (0, 128) if h == 0 else (512, 64)
        sums = []
        for k, gap in enumerate(gaps):
            rows = slice(low + size * k, low + size * (k + 1))
            w = jnp.exp2((work.s[buf, rows] - (top[:1] + gap)) * LOG2)
            sums.append(fold(w, jnp.sum))
            work.p[buf, rows] = w.astype(jnp.bfloat16)
        total = sum(sums)
        work.m[q, h] = top
        work.l[q, h] = total if first else work.l[q, h] * factor + total


def gather(work, buf, q, js, first=False):
    for h, rows in enumerate((slice(0, 512), slice(512, 768))):
        out = jnp.dot(values_of(work.kv, js, h), work.p[buf, rows], preferred_element_type=jnp.float32)
        work.acc[q, h] = out if first else work.acc[q, h] * work.factor[buf, h, 0:1] + out


def pipelined(score, soft, add, rounds, unroll=UNROLL):
    score(0, 0)
    score(1, 1)
    soft(0, 0)

    def body(i, carry):
        for k in range(unroll):
            t = unroll * i + k
            score(t + 2, k % 2)
            add(t, k % 2)
            soft(t + 1, (k + 1) % 2)
        return carry

    lax.fori_loop(0, rounds, body, 0)


def run_list(work, list_ref, steps):
    def score(t, buf):
        q, js, _ = slots(list_ref, t)
        scores(work, buf, q, js)

    def soft(t, buf):
        q, _, gaps = slots(list_ref, t)
        soften(work, buf, q, gaps)

    def add(t, buf):
        q, js, _ = slots(list_ref, t)
        gather(work, buf, q, js)

    pipelined(score, soft, add, (steps + UNROLL - 1) // UNROLL)


def own_kernel(
    first_ref, rest_ref, n_ref, live_ref, kv_hbm, text_hbm, q_hbm, other_hbm,
    acc_ref, m_ref, l_ref, kv_ref, q_ref, s_ref, p_ref, t_ref, f_ref, sems,
):
    copies = [
        pltpu.make_async_copy(kv_hbm, kv_ref.at[pl.ds(0, HALF)], sems.at[0]),
        pltpu.make_async_copy(text_hbm, kv_ref.at[pl.ds(HALF, 1)], sems.at[1]),
        pltpu.make_async_copy(q_hbm, q_ref.at[pl.ds(0, HALF)], sems.at[2]),
        pltpu.make_async_copy(other_hbm, q_ref.at[pl.ds(HALF, HALF)], sems.at[3]),
    ]
    work = Work(kv_ref, q_ref, s_ref, p_ref, t_ref, f_ref, acc_ref, m_ref, l_ref)
    for copy in copies:
        copy.start()
    for copy in copies:
        copy.wait()

    def line(n):
        codes = [first_ref[STEP * n + k] for k in range(STEP - 1)]
        gaps = [jnp.float32(0)]
        gaps += [jnp.where(code >= FLAG, jnp.float32(1e30), jnp.float32(0)) for code in codes]
        return [jnp.int32(HALF)] + [code & 63 for code in codes], gaps

    def score(n, buf):
        n = jnp.minimum(n, SLAB - 1)
        scores(work, buf, n, line(n)[0], (live_ref[0], live_ref[1]))

    def soft(n, buf):
        n = jnp.minimum(n, SLAB - 1)
        soften(work, buf, n, line(n)[1], True)

    def add(n, buf):
        gather(work, buf, n, line(n)[0], True)

    pipelined(score, soft, add, SLAB // 16, 16)
    run_list(work, rest_ref, n_ref[0])


def text_kernel(
    live_ref, kv_ref, text_ref, q_ref, out_ref, s_ref, p_ref, t_ref, f_ref, acc_ref, m_ref, l_ref
):
    none = [jnp.float32(0)] * STEP
    live = (live_ref[2], live_ref[3])
    work = Work(kv_ref, q_ref, s_ref, p_ref, t_ref, f_ref, acc_ref, m_ref, l_ref)

    for start in range(0, HALF, STEP):
        js = list(range(start, start + STEP))
        for block in range(NTQ):
            scores(work, block, block, js)
        for block in range(NTQ):
            soften(work, block, block, none, start == 0)
        for block in range(NTQ):
            gather(work, block, block, js, start == 0)
    for block in range(NTQ):
        for h, (low, size, row) in enumerate(((0, 128, 0), (512, 64, 128))):
            s = jnp.dot(
                text_ref[0, row : row + size],
                q_ref[block, 128 * h : 128 * h + 128],
                preferred_element_type=jnp.float32,
            )
            rows = lax.broadcasted_iota(jnp.int32, s.shape, 0)
            s = jnp.where(rows < live[h], s, neg_fill)
            old = m_ref[block, h]
            new = jnp.maximum(old, column_max(s))
            factor = jnp.exp2((old - new) * LOG2)
            w = jnp.exp2((s - new[:1]) * LOG2)
            total = row_sum(l_ref[block, h] * factor) + row_sum(fold(w, jnp.sum))
            v = text_ref[0, 192:320] if h == 0 else wide_c(text_ref, [0])
            acc = acc_ref[block, h] * factor[:1] + jnp.dot(
                v, w.astype(jnp.bfloat16), preferred_element_type=jnp.float32
            )
            put_text(out_ref, h * NTQ + block, new[:1], total, acc)


def row_sum(x):
    return jnp.sum(x, axis=0, keepdims=True)


def put_text(ref, at, top, total, acc):
    ref[at, 0:128] = acc.astype(jnp.bfloat16)
    ref[at, 128:144] = stat_rows([top, total])


def merged(blocks):
    stats = [stats_of(block[128:144], 2) for block in blocks]
    top = functools.reduce(jnp.maximum, [s[0] for s in stats])
    factors = [jnp.exp2((s[0] - top) * LOG2) for s in stats]
    total = sum(s[1] * f for s, f in zip(stats, factors))
    return top, total, sum(b[0:128].astype(jnp.float32) * f for b, f in zip(blocks, factors))


def merge_text_kernel(member_ref, here_ref, there_ref, out_ref):
    first = member_ref[0] == 0
    rows = 2 * NTQ
    for block in range(NTQ):
        for head in range(3):
            at = (0 if head < 2 else NTQ) + block
            pairs = [(here_ref[core * rows + at], there_ref[core * rows + at]) for core in range(2)]
            if head == 2:
                blocks = [part for both in pairs for part in both]
            else:
                ours = first if head == 0 else jnp.logical_not(first)
                blocks = [jnp.where(ours, *both) for both in pairs]
            put_text(out_ref, head * NTQ + block, *merged(blocks))


def final_text_kernel(*refs):
    for block in range(NTQ):
        for head in range(3):
            _, total, acc = merged([ref[head * NTQ + block] for ref in refs[:-1]])
            out = (acc / total).astype(jnp.bfloat16).T
            refs[-1][128 * block : 128 * block + 128, head * DH : head * DH + DH] = out


def split3(x):
    rows = []
    for _ in range(3):
        part = x.astype(jnp.bfloat16)
        rows.append(part)
        x = x - part.astype(jnp.float32)
    return rows


def stat_rows(rows):
    parts = [part for row in rows for part in split3(row)]
    pad = jnp.zeros((16 - len(parts), DH), jnp.bfloat16)
    return jnp.concatenate(parts + [pad], axis=0)


def stats_of(block, count):
    x = block.astype(jnp.float32)
    return [x[3 * i : 3 * i + 1] + x[3 * i + 1 : 3 * i + 2] + x[3 * i + 2 : 3 * i + 3] for i in range(count)]


def halo_kernel(
    which, list_ref, n_ref, down_hbm, up_hbm, q_hbm, acc_hbm, m_hbm, l_hbm,
    *refs,
):
    if which == 0:
        out_ref, kv_ref, q_ref, s_ref, p_ref, t_ref, f_ref, acc_ref, m_ref, l_ref, sems = refs
    else:
        acc_ref, m_ref, l_ref, kv_ref, q_ref, s_ref, p_ref, t_ref, f_ref, sems = refs
    base = HALF if which == 0 else 0
    copies = [
        pltpu.make_async_copy(down_hbm, kv_ref.at[pl.ds(0, HALF)], sems.at[0]),
        pltpu.make_async_copy(up_hbm, kv_ref.at[pl.ds(HALF, HALF)], sems.at[1]),
        pltpu.make_async_copy(q_hbm, q_ref.at[pl.ds(0, HALF)], sems.at[2]),
        pltpu.make_async_copy(acc_hbm.at[pl.ds(base, HALF)], acc_ref.at[pl.ds(0, HALF)], sems.at[3]),
        pltpu.make_async_copy(m_hbm.at[pl.ds(base, HALF)], m_ref.at[pl.ds(0, HALF)], sems.at[4]),
        pltpu.make_async_copy(l_hbm.at[pl.ds(base, HALF)], l_ref.at[pl.ds(0, HALF)], sems.at[5]),
    ]
    for copy in copies:
        copy.start()
    for copy in copies:
        copy.wait()
    work = Work(kv_ref, q_ref, s_ref, p_ref, t_ref, f_ref, acc_ref, m_ref, l_ref)
    run_list(work, list_ref, n_ref[1 + which])
    if which == 0:

        def finish(n, carry):
            rows = []
            for h in range(2):
                out_ref[n, 128 * h : 128 * h + 128] = acc_ref[n, h].astype(jnp.bfloat16)
                rows += [m_ref[n, h, 0:1], jnp.sum(l_ref[n, h], axis=0, keepdims=True)]
            out_ref[n, 256:272] = stat_rows(rows)
            return carry

        lax.fori_loop(0, HALF, finish, 0)


def merge_kernel(acc_ref, m_ref, l_ref, got_ref, out_ref):
    def one(n, carry):
        stats = stats_of(got_ref[n, 256:272], 4)
        for h in range(2):
            mine, ours = m_ref[n, h, 0:1], jnp.sum(l_ref[n, h], axis=0, keepdims=True)
            his, theirs = stats[2 * h], stats[2 * h + 1]
            top = jnp.maximum(mine, his)
            a, b = jnp.exp2((mine - top) * LOG2), jnp.exp2((his - top) * LOG2)
            total = ours * a + theirs * b
            acc = acc_ref[n, h] * a + got_ref[n, 128 * h : 128 * h + 128].astype(jnp.float32) * b
            if h == 0:
                out_ref[n, 0:128] = (acc / total).astype(jnp.bfloat16)
            else:
                out_ref[n, 128:256] = acc.astype(jnp.bfloat16)
                out_ref[n, 256:272] = stat_rows([top, total])
        return carry

    lax.fori_loop(0, HALF, one, 0)


def final_kernel(got_ref, out_ref):
    for x in range(4):
        for pair in range(2):
            first, second = 4 * (2 * pair) + x, 4 * (2 * pair + 1) + x
            col = (6 * x + 3 * pair) * DH
            out_ref[:, col : col + DH] = got_ref[first, 0:128].T
            out_ref[:, col + DH : col + 2 * DH] = got_ref[second, 0:128].T
            m1, l1 = stats_of(got_ref[first, 256:272], 2)
            m2, l2 = stats_of(got_ref[second, 256:272], 2)
            top = jnp.maximum(m1, m2)
            a, b = jnp.exp2((m1 - top) * LOG2), jnp.exp2((m2 - top) * LOG2)
            total = l1 * a + l2 * b
            acc = got_ref[first, 128:256].astype(jnp.float32) * a
            acc = (acc + got_ref[second, 128:256].astype(jnp.float32) * b) / total
            out_ref[:, col + 2 * DH : col + 3 * DH] = acc.astype(jnp.bfloat16).T


def ring(x, axis):
    routes = [[(i, (i + far) % 4) for i in range(4)] for far in (1, 2, 3)]
    return [x] + [lax.ppermute(x, axis, route) for route in routes]


def shape(dims, dtype=jnp.bfloat16):
    return jax.ShapeDtypeStruct(dims, dtype)


def state(n):
    return [shape((n, 2, 128, 128), jnp.float32)] + [shape((n, 2, 8, 128), jnp.float32)] * 2


def run_lists(place, block_mask):
    return pl.pallas_call(
        lists_kernel,
        out_shape=[shape((n,), jnp.int32) for n in (FIRST_LEN, REST_LEN, HALO_LEN, HALO_LEN, 4)],
        in_specs=[SM, SM],
        out_specs=[SM] * 5,
        compiler_params=PARAMS,
        cost_estimate=pl.CostEstimate(flops=8 * 10**9, bytes_accessed=10**5, transcendentals=0),
        name="lists",
    )(place, block_mask)


def run_own(first, rest, counts, live, kv, text_rec, q, q_other):
    return pl.pallas_call(
        own_kernel,
        out_shape=state(SLAB + 1),
        in_specs=[SM] * 4 + [ANY] * 4,
        out_specs=[VM] * 3,
        scratch_shapes=[
            pltpu.VMEM((HALF + 1, REC, DH), jnp.bfloat16),
            pltpu.VMEM((SLAB + 1, QREC, DH), jnp.bfloat16),
            pltpu.VMEM((2, 768, DH), jnp.float32),
            pltpu.VMEM((2, 768, DH), jnp.bfloat16),
            pltpu.VMEM((2, 2, 8, DH), jnp.float32),
            pltpu.VMEM((2, 2, 8, DH), jnp.float32),
            pltpu.SemaphoreType.DMA((4,)),
        ],
        compiler_params=PARAMS,
        cost_estimate=pl.CostEstimate(flops=10**8, bytes_accessed=10**6, transcendentals=0),
        name="own_keys",
    )(first, rest, counts, live, kv, text_rec, q, q_other)


def run_text(live, kv, text_rec, tq):
    scratch = [pltpu.VMEM((NTQ, 768, DH), jnp.float32), pltpu.VMEM((NTQ, 768, DH), jnp.bfloat16)]
    scratch += [pltpu.VMEM((NTQ, 2, 8, DH), jnp.float32)] * 2
    return pl.pallas_call(
        text_kernel,
        out_shape=shape((2 * NTQ, 144, DH)),
        in_specs=[SM] + [VM] * 3,
        out_specs=VM,
        scratch_shapes=scratch + [pltpu.VMEM(s.shape, jnp.float32) for s in state(NTQ)],
        compiler_params=PARAMS,
        cost_estimate=pl.CostEstimate(flops=10**7, bytes_accessed=10**5, transcendentals=0),
        name="text_keys",
    )(live, kv, text_rec, tq)


def run_halo(which, queries, table, counts, from_down, from_up, acc, m, l):
    scratch = [
        pltpu.VMEM((SLAB, REC, DH), jnp.bfloat16),
        pltpu.VMEM((HALF + 1, QREC, DH), jnp.bfloat16),
        pltpu.VMEM((2, 768, DH), jnp.float32),
        pltpu.VMEM((2, 768, DH), jnp.bfloat16),
        pltpu.VMEM((2, 2, 8, DH), jnp.float32),
        pltpu.VMEM((2, 2, 8, DH), jnp.float32),
    ]
    if which == 0:
        out = shape((HALF, OREC, DH))
        scratch += [pltpu.VMEM(s.shape, jnp.float32) for s in state(HALF + 1)]
    else:
        out = state(HALF + 1)
    return pl.pallas_call(
        functools.partial(halo_kernel, which),
        out_shape=out,
        in_specs=[SM, SM] + [ANY] * 6,
        out_specs=VM if which == 0 else [VM] * 3,
        scratch_shapes=scratch + [pltpu.SemaphoreType.DMA((6,))],
        compiler_params=PARAMS,
        cost_estimate=pl.CostEstimate(flops=2 * 10**9, bytes_accessed=10**7, transcendentals=4 * 10**6),
        name="halo_keys",
    )(table, counts, from_down, from_up, queries, acc, m, l)


def local(video_q, video_k, video_v, text_q, text_k, text_v, block_mask, text_count):
    f32 = jnp.float32
    together = lax.optimization_barrier
    y, z, c = lax.axis_index("y"), lax.axis_index("z"), lax.axis_index("c")
    pair, member = z // 2, z % 2
    chips = ("z", "x")
    swap = [(0, 1), (1, 0)]

    kv_send = pl.pallas_call(
        prep_kv_kernel, out_shape=shape((16, REC, DH)), in_specs=[ANY] * 2, out_specs=VM,
        scratch_shapes=[pltpu.VMEM((BLOCK, 24 * DH), jnp.bfloat16)] * 2 + [pltpu.SemaphoreType.DMA((6,))],
        compiler_params=pltpu.CompilerParams(vmem_limit_bytes=60 << 20), name="prep_kv",
    )(video_k, video_v)
    kv = lax.all_to_all(kv_send, chips, 0, 0, tiled=True)

    text_q, text_k, text_v, block_mask, _ = together((text_q, text_k, text_v, block_mask, kv_send))
    text = jnp.stack([text_q, text_k, text_v])
    text = jnp.where(c == pair, text, lax.ppermute(text, "c", swap))
    head = lax.dynamic_slice_in_dim(text, member * DH, DH, 2)
    shared = text[:, :, 2 * DH :]
    tq = jnp.stack([head[0].T, shared[0].T])
    tq = tq.reshape(2, DH, NTQ, DH).transpose(2, 0, 1, 3).reshape(NTQ, QREC, DH)
    mine = lax.dynamic_slice_in_dim(head, c * BLOCK, BLOCK, 1)
    half = lax.dynamic_slice_in_dim(shared, c * BLOCK + member * 64, 64, 1)
    vt = half[2].T
    text_rec = jnp.concatenate(
        [mine[1], half[1], mine[2].T, jnp.concatenate([vt[:64], vt[64:]], axis=1)], axis=0
    )[None]
    live_a = jnp.clip(text_count[0] - c * BLOCK, 0, BLOCK)
    live_c = jnp.clip(text_count[0] - c * BLOCK - member * 64, 0, 64)
    lead = y == 0
    live = jnp.stack([live_a, live_c, jnp.where(lead, live_a, 0), jnp.where(lead, live_c, 0)])
    live = live.astype(jnp.int32)
    place = jnp.stack([y, c]).astype(jnp.int32)
    first, rest, halo_a, halo_b, counts = run_lists(place, block_mask)
    video_q, tq, text_rec, first, rest, halo_a, halo_b, counts = together(
        (video_q, tq, text_rec, first, rest, halo_a, halo_b, counts)
    )
    q_send = pl.pallas_call(
        prep_q_kernel, out_shape=shape((16, QREC, DH)), in_specs=[VM], out_specs=VM,
        compiler_params=PARAMS, name="prep_q",
    )(video_q)

    q_send, kv = together((q_send, kv))
    from_down = lax.ppermute(kv, "y", [(0, 1), (1, 2), (2, 3)])
    from_up = lax.ppermute(kv, "y", [(1, 0), (2, 1), (3, 2)])
    q = lax.all_to_all(q_send, chips, 0, 0, tiled=True)
    text_part = run_text(live, kv, text_rec, tq)
    here = jnp.concatenate([text_part, lax.ppermute(text_part, "c", swap)])
    q, here = together((q, here))
    q_other = lax.ppermute(q, "c", swap)
    there = lax.ppermute(here, "z", [(0, 1), (1, 0), (2, 3), (3, 2)])
    acc, m, l = run_own(first, rest, counts, live, kv, text_rec, q, q_other)
    acc, there = together((acc, there))
    heads = pl.pallas_call(
        merge_text_kernel, out_shape=shape((3 * NTQ, 144, DH)), in_specs=[SM, VM, VM], out_specs=VM,
        compiler_params=PARAMS, name="merge_text",
    )(member.astype(jnp.int32)[None], here, there)
    acc, heads = together((acc, heads))
    far = lax.ppermute(heads, "z", [(0, 2), (1, 3), (2, 0), (3, 1)])
    heads = jnp.where(c == pair, heads, far)

    partial = run_halo(0, q_other, halo_a, counts, from_down, from_up, acc, m, l)
    got = lax.ppermute(partial, "c", swap)
    acc2, m2, l2 = run_halo(1, q, halo_b, counts, from_down, from_up, acc, m, l)
    got, heads = together((got, heads))
    record = pl.pallas_call(
        merge_kernel, out_shape=shape((HALF, OREC, DH)), in_specs=[VM] * 4, out_specs=VM,
        compiler_params=PARAMS, name="merge_cores",
    )(acc2, m2, l2, got)
    back = lax.all_to_all(record, chips, 0, 0, tiled=True)
    heads, _ = together((heads, record))
    text_out = pl.pallas_call(
        final_text_kernel, out_shape=shape((TEXT, 3 * DH)), in_specs=[VM] * 4, out_specs=VM,
        compiler_params=PARAMS, name="final_text",
    )(*ring(heads, "y"))
    video_out = pl.pallas_call(
        final_kernel, out_shape=shape((BLOCK, 24 * DH)), in_specs=[VM], out_specs=VM,
        compiler_params=PARAMS, name="final",
    )(back)
    return video_out, text_out


def solution(mesh):
    grid = Mesh(mesh.devices.reshape(4, 4, 4, 2), ("y", "z", "x", "c"))
    video = P(("y", "z", "x", "c"), None)
    text = P(None, ("x", "c"))
    return jax.shard_map(
        local,
        mesh=grid,
        in_specs=(video, video, video, text, text, text, P(), P()),
        out_specs=(video, text),
        check_vma=False,
    )
```

```python
import functools

import jax
import jax.numpy as jnp
import numpy as np
from jax import lax
from jax.experimental import pallas as pl
from jax.experimental.pallas import tpu as pltpu
from jax.sharding import Mesh, PartitionSpec as P

DH = 128
TEXT = 256
BLOCK = 128
SLAB = 32
HALF = 16
NTQ = 2
REC = 384
QREC = 256
OREC = 272
STEP = 4
UNROLL = 8
LOG2 = float(DH**-0.5 * np.log2(np.e))
neg_fill = -1e30
FLAG = 4096
FIRST_LEN = SLAB * STEP
PAD = (UNROLL + 2) * STEP
REST_LEN = SLAB * (HALF + STEP) + PAD
HALO_LEN = HALF * (2 * HALF + STEP) + PAD

VM = pl.BlockSpec(memory_space=pltpu.VMEM)
SM = pl.BlockSpec(memory_space=pltpu.SMEM)
ANY = pl.BlockSpec(memory_space=pl.ANY)
PARAMS = pltpu.CompilerParams(vmem_limit_bytes=20 << 20)


def head_a(chip):
    z, x = chip // 4, chip % 4
    return 6 * x + 3 * (z // 2) + z % 2


def head_c(chip):
    z, x = chip // 4, chip % 4
    return 6 * x + 3 * (z // 2) + 2


def packed(vt, half):
    cols = vt[:, 64 * half : 64 * half + 64]
    return jnp.concatenate([cols[:64], cols[64:]], axis=1)


def prep_kv_kernel(k_hbm, v_hbm, out_ref, k_ref, v_ref, sems):
    third = 8 * DH
    copies = [
        [
            pltpu.make_async_copy(
                hbm.at[:, pl.ds(third * i, third)], ref.at[:, pl.ds(third * i, third)], sems.at[2 * i + j]
            )
            for j, (hbm, ref) in enumerate(((k_hbm, k_ref), (v_hbm, v_ref)))
        ]
        for i in range(3)
    ]
    for pair in copies:
        for copy in pair:
            copy.start()
    arrived = 0
    for x in range(4):
        while 8 * arrived < 6 * (x + 1):
            for copy in copies[arrived]:
                copy.wait()
            arrived += 1
        for z in range(4):
            chip = 4 * z + x
            a, c, half = head_a(chip) * DH, head_c(chip) * DH, z % 2
            out_ref[chip, 0:128] = k_ref[:, a : a + DH]
            out_ref[chip, 128:192] = k_ref[64 * half : 64 * half + 64, c : c + DH]
            out_ref[chip, 192:320] = v_ref[:, a : a + DH].T
            out_ref[chip, 320:384] = packed(v_ref[:, c : c + DH].T, half)


def prep_q_kernel(q_ref, out_ref):
    for chip in range(16):
        a, c = head_a(chip) * DH, head_c(chip) * DH
        out_ref[chip, 0:128] = q_ref[:, a : a + DH].T
        out_ref[chip, 128:256] = q_ref[:, c : c + DH].T


def lists_kernel(place_ref, mask_ref, first_ref, rest_ref, halo_a_ref, halo_b_ref, n_ref):
    y, c = place_ref[0], place_ref[1]

    def kept(q, j, dy):
        col = (y + dy) * SLAB + 2 * j + c
        inside = jnp.logical_and(col >= 0, col < 4 * SLAB)
        value = mask_ref[y * SLAB + q, jnp.clip(col, 0, 4 * SLAB - 1)]
        return jnp.where(inside, value, 0)

    def row_of(n):
        return jnp.where(n < HALF, 2 * n + c, 2 * (n - HALF) + 1 - c)

    def close(ref, start, pos, size):
        last = ref[jnp.maximum(pos - 1, 0)]
        for _ in range(size - 1):
            missing = (pos - start) % size != 0

            @pl.when(missing)
            def _():
                ref[pos] = last | FLAG

            pos = pos + jnp.where(missing, 1, 0)
        return pos

    def own(n, pos):
        row = row_of(n)
        count = jnp.int32(0)
        start = pos
        for j in range(HALF):
            hit = kept(row, j, 0)

            @pl.when(jnp.logical_and(hit > 0, count < STEP - 1))
            def _():
                first_ref[n * STEP + count] = n * 64 + j

            @pl.when(jnp.logical_and(hit > 0, count >= STEP - 1))
            def _():
                rest_ref[pos] = n * 64 + j

            pos = pos + jnp.where(jnp.logical_and(hit > 0, count >= STEP - 1), 1, 0)
            count = count + hit
        some = jnp.minimum(count, STEP - 1)
        last = jnp.where(some > 0, first_ref[n * STEP + jnp.maximum(some - 1, 0)], n * 64)
        for k in range(STEP):

            @pl.when(k >= some)
            def _():
                first_ref[n * STEP + k] = last | FLAG

        return close(rest_ref, start, pos, STEP)

    end = lax.fori_loop(0, SLAB, own, jnp.int32(0))
    n_ref[0] = end // STEP
    for k in range(PAD):
        rest_ref[end + k] = FLAG | SLAB * 64
    for which, (ref, base) in enumerate(((halo_a_ref, HALF), (halo_b_ref, 0))):

        def far(n, pos):
            start = pos
            row = row_of(n + base)
            for dy, shift in ((-1, 0), (1, HALF)):
                for j in range(HALF):
                    hit = kept(row, j, dy)

                    @pl.when(hit > 0)
                    def _():
                        ref[pos] = n * 64 + shift + j

                    pos = pos + hit
            return close(ref, start, pos, STEP)

        end = lax.fori_loop(0, HALF, far, jnp.int32(0))
        n_ref[1 + which] = end // STEP
        for k in range(PAD):
            ref[end + k] = FLAG | HALF * 64
    n_ref[3] = 0


def fold(x, op):
    return op(x.reshape(-1, 8, DH), axis=0)


def slots(list_ref, t):
    codes = [list_ref[STEP * t + k] for k in range(STEP)]
    q = (codes[0] & (FLAG - 1)) >> 6
    gaps = [jnp.where(code >= FLAG, jnp.float32(1e30), jnp.float32(0)) for code in codes]
    return q, [code & 63 for code in codes], gaps


def wide_c(kv_ref, js):
    low, high = [], []
    for j in js:
        part = kv_ref[j, 320:384]
        low.append(part[:, :64])
        high.append(part[:, 64:])
    return jnp.concatenate([jnp.concatenate(low, axis=1), jnp.concatenate(high, axis=1)], axis=0)


class Work:
    def __init__(self, kv, q, s, p, top, factor, acc, m, l):
        self.kv, self.q, self.s, self.p, self.top, self.factor = kv, q, s, p, top, factor
        self.acc, self.m, self.l = acc, m, l


def scores(work, buf, q, js, live=None):
    for h, (low, size, row) in enumerate(((0, 128, 0), (512, 64, 128))):
        keys = jnp.concatenate([work.kv[j, row : row + size] for j in js], axis=0)
        s = jnp.dot(keys, work.q[q, 128 * h : 128 * h + 128], preferred_element_type=jnp.float32)
        if live is not None:
            rows = lax.broadcasted_iota(jnp.int32, (size, DH), 0)
            s = jnp.concatenate([jnp.where(rows < live[h], s[:size], neg_fill), s[size:]], axis=0)
        work.s[buf, low : low + STEP * size] = s
        work.top[buf, h] = jnp.broadcast_to(column_max(s), (8, DH))


def column_max(s):
    return jnp.max(fold(s, jnp.max), axis=0, keepdims=True)


def values_of(kv_ref, js, h):
    if h == 0:
        return jnp.concatenate([kv_ref[j, 192:320] for j in js], axis=1)
    return wide_c(kv_ref, js)


def soften(work, buf, q, gaps, first=False):
    for h in range(2):
        top = work.top[buf, h]
        if not first:
            old = work.m[q, h]
            top = jnp.maximum(old, top)
            factor = jnp.exp2((old - top) * LOG2)
            work.factor[buf, h] = factor
        low, size = (0, 128) if h == 0 else (512, 64)
        sums = []
        for k, gap in enumerate(gaps):
            rows = slice(low + size * k, low + size * (k + 1))
            w = jnp.exp2((work.s[buf, rows] - (top[:1] + gap)) * LOG2)
            sums.append(fold(w, jnp.sum))
            work.p[buf, rows] = w.astype(jnp.bfloat16)
        total = sum(sums)
        work.m[q, h] = top
        work.l[q, h] = total if first else work.l[q, h] * factor + total


def gather(work, buf, q, js, first=False):
    for h, rows in enumerate((slice(0, 512), slice(512, 768))):
        out = jnp.dot(values_of(work.kv, js, h), work.p[buf, rows], preferred_element_type=jnp.float32)
        work.acc[q, h] = out if first else work.acc[q, h] * work.factor[buf, h, 0:1] + out


def pipelined(score, soft, add, rounds, unroll=UNROLL):
    score(0, 0)
    score(1, 1)
    soft(0, 0)

    def body(i, carry):
        for k in range(unroll):
            t = unroll * i + k
            score(t + 2, k % 2)
            add(t, k % 2)
            soft(t + 1, (k + 1) % 2)
        return carry

    lax.fori_loop(0, rounds, body, 0)


def run_list(work, list_ref, steps):
    def score(t, buf):
        q, js, _ = slots(list_ref, t)
        scores(work, buf, q, js)

    def soft(t, buf):
        q, _, gaps = slots(list_ref, t)
        soften(work, buf, q, gaps)

    def add(t, buf):
        q, js, _ = slots(list_ref, t)
        gather(work, buf, q, js)

    pipelined(score, soft, add, (steps + UNROLL - 1) // UNROLL)


def own_kernel(
    first_ref, rest_ref, n_ref, live_ref, kv_hbm, text_hbm, q_hbm, other_hbm,
    acc_ref, m_ref, l_ref, kv_ref, q_ref, s_ref, p_ref, t_ref, f_ref, sems,
):
    copies = [
        pltpu.make_async_copy(kv_hbm, kv_ref.at[pl.ds(0, HALF)], sems.at[0]),
        pltpu.make_async_copy(text_hbm, kv_ref.at[pl.ds(HALF, 1)], sems.at[1]),
        pltpu.make_async_copy(q_hbm, q_ref.at[pl.ds(0, HALF)], sems.at[2]),
        pltpu.make_async_copy(other_hbm, q_ref.at[pl.ds(HALF, HALF)], sems.at[3]),
    ]
    work = Work(kv_ref, q_ref, s_ref, p_ref, t_ref, f_ref, acc_ref, m_ref, l_ref)
    for copy in copies:
        copy.start()
    for copy in copies:
        copy.wait()

    def line(n):
        codes = [first_ref[STEP * n + k] for k in range(STEP - 1)]
        gaps = [jnp.float32(0)]
        gaps += [jnp.where(code >= FLAG, jnp.float32(1e30), jnp.float32(0)) for code in codes]
        return [jnp.int32(HALF)] + [code & 63 for code in codes], gaps

    def score(n, buf):
        n = jnp.minimum(n, SLAB - 1)
        scores(work, buf, n, line(n)[0], (live_ref[0], live_ref[1]))

    def soft(n, buf):
        n = jnp.minimum(n, SLAB - 1)
        soften(work, buf, n, line(n)[1], True)

    def add(n, buf):
        gather(work, buf, n, line(n)[0], True)

    pipelined(score, soft, add, SLAB // 16, 16)
    run_list(work, rest_ref, n_ref[0])


def text_kernel(
    live_ref, kv_ref, text_ref, q_ref, out_ref, s_ref, p_ref, t_ref, f_ref, acc_ref, m_ref, l_ref
):
    none = [jnp.float32(0)] * STEP
    live = (live_ref[2], live_ref[3])
    work = Work(kv_ref, q_ref, s_ref, p_ref, t_ref, f_ref, acc_ref, m_ref, l_ref)

    for start in range(0, HALF, STEP):
        js = list(range(start, start + STEP))
        for block in range(NTQ):
            scores(work, block, block, js)
        for block in range(NTQ):
            soften(work, block, block, none, start == 0)
        for block in range(NTQ):
            gather(work, block, block, js, start == 0)
    for block in range(NTQ):
        for h, (low, size, row) in enumerate(((0, 128, 0), (512, 64, 128))):
            s = jnp.dot(
                text_ref[0, row : row + size],
                q_ref[block, 128 * h : 128 * h + 128],
                preferred_element_type=jnp.float32,
            )
            rows = lax.broadcasted_iota(jnp.int32, s.shape, 0)
            s = jnp.where(rows < live[h], s, neg_fill)
            old = m_ref[block, h]
            new = jnp.maximum(old, column_max(s))
            factor = jnp.exp2((old - new) * LOG2)
            w = jnp.exp2((s - new[:1]) * LOG2)
            total = row_sum(l_ref[block, h] * factor) + row_sum(fold(w, jnp.sum))
            v = text_ref[0, 192:320] if h == 0 else wide_c(text_ref, [0])
            acc = acc_ref[block, h] * factor[:1] + jnp.dot(
                v, w.astype(jnp.bfloat16), preferred_element_type=jnp.float32
            )
            put_text(out_ref, h * NTQ + block, new[:1], total, acc)


def row_sum(x):
    return jnp.sum(x, axis=0, keepdims=True)


def put_text(ref, at, top, total, acc):
    ref[at, 0:128] = acc.astype(jnp.bfloat16)
    ref[at, 128:144] = stat_rows([top, total])


def merged(blocks):
    stats = [stats_of(block[128:144], 2) for block in blocks]
    top = functools.reduce(jnp.maximum, [s[0] for s in stats])
    factors = [jnp.exp2((s[0] - top) * LOG2) for s in stats]
    total = sum(s[1] * f for s, f in zip(stats, factors))
    return top, total, sum(b[0:128].astype(jnp.float32) * f for b, f in zip(blocks, factors))


def merge_text_kernel(member_ref, here_ref, there_ref, out_ref):
    first = member_ref[0] == 0
    rows = 2 * NTQ
    for block in range(NTQ):
        for head in range(3):
            at = (0 if head < 2 else NTQ) + block
            pairs = [(here_ref[core * rows + at], there_ref[core * rows + at]) for core in range(2)]
            if head == 2:
                blocks = [part for both in pairs for part in both]
            else:
                ours = first if head == 0 else jnp.logical_not(first)
                blocks = [jnp.where(ours, *both) for both in pairs]
            put_text(out_ref, head * NTQ + block, *merged(blocks))


def final_text_kernel(*refs):
    for block in range(NTQ):
        for head in range(3):
            _, total, acc = merged([ref[head * NTQ + block] for ref in refs[:-1]])
            out = (acc / total).astype(jnp.bfloat16).T
            refs[-1][128 * block : 128 * block + 128, head * DH : head * DH + DH] = out


def split3(x):
    rows = []
    for _ in range(3):
        part = x.astype(jnp.bfloat16)
        rows.append(part)
        x = x - part.astype(jnp.float32)
    return rows


def stat_rows(rows):
    parts = [part for row in rows for part in split3(row)]
    pad = jnp.zeros((16 - len(parts), DH), jnp.bfloat16)
    return jnp.concatenate(parts + [pad], axis=0)


def stats_of(block, count):
    x = block.astype(jnp.float32)
    return [x[3 * i : 3 * i + 1] + x[3 * i + 1 : 3 * i + 2] + x[3 * i + 2 : 3 * i + 3] for i in range(count)]


def halo_kernel(
    which, list_ref, n_ref, down_hbm, up_hbm, q_hbm, acc_hbm, m_hbm, l_hbm,
    *refs,
):
    if which == 0:
        out_ref, kv_ref, q_ref, s_ref, p_ref, t_ref, f_ref, acc_ref, m_ref, l_ref, sems = refs
    else:
        acc_ref, m_ref, l_ref, kv_ref, q_ref, s_ref, p_ref, t_ref, f_ref, sems = refs
    base = HALF if which == 0 else 0
    copies = [
        pltpu.make_async_copy(down_hbm, kv_ref.at[pl.ds(0, HALF)], sems.at[0]),
        pltpu.make_async_copy(up_hbm, kv_ref.at[pl.ds(HALF, HALF)], sems.at[1]),
        pltpu.make_async_copy(q_hbm, q_ref.at[pl.ds(0, HALF)], sems.at[2]),
        pltpu.make_async_copy(acc_hbm.at[pl.ds(base, HALF)], acc_ref.at[pl.ds(0, HALF)], sems.at[3]),
        pltpu.make_async_copy(m_hbm.at[pl.ds(base, HALF)], m_ref.at[pl.ds(0, HALF)], sems.at[4]),
        pltpu.make_async_copy(l_hbm.at[pl.ds(base, HALF)], l_ref.at[pl.ds(0, HALF)], sems.at[5]),
    ]
    for copy in copies:
        copy.start()
    for copy in copies:
        copy.wait()
    work = Work(kv_ref, q_ref, s_ref, p_ref, t_ref, f_ref, acc_ref, m_ref, l_ref)
    run_list(work, list_ref, n_ref[1 + which])
    if which == 0:

        def finish(n, carry):
            rows = []
            for h in range(2):
                out_ref[n, 128 * h : 128 * h + 128] = acc_ref[n, h].astype(jnp.bfloat16)
                rows += [m_ref[n, h, 0:1], jnp.sum(l_ref[n, h], axis=0, keepdims=True)]
            out_ref[n, 256:272] = stat_rows(rows)
            return carry

        lax.fori_loop(0, HALF, finish, 0, unroll=8)


def merge_kernel(acc_ref, m_ref, l_ref, got_ref, out_ref):
    def one(n, carry):
        stats = stats_of(got_ref[n, 256:272], 4)
        for h in range(2):
            mine, ours = m_ref[n, h, 0:1], jnp.sum(l_ref[n, h], axis=0, keepdims=True)
            his, theirs = stats[2 * h], stats[2 * h + 1]
            top = jnp.maximum(mine, his)
            a, b = jnp.exp2((mine - top) * LOG2), jnp.exp2((his - top) * LOG2)
            total = ours * a + theirs * b
            acc = acc_ref[n, h] * a + got_ref[n, 128 * h : 128 * h + 128].astype(jnp.float32) * b
            if h == 0:
                out_ref[n, 0:128] = (acc / total).astype(jnp.bfloat16)
            else:
                out_ref[n, 128:256] = acc.astype(jnp.bfloat16)
                out_ref[n, 256:272] = stat_rows([top, total])
        return carry

    lax.fori_loop(0, HALF, one, 0, unroll=8)


def final_kernel(got_ref, out_ref):
    for x in range(4):
        for pair in range(2):
            first, second = 4 * (2 * pair) + x, 4 * (2 * pair + 1) + x
            col = (6 * x + 3 * pair) * DH
            out_ref[:, col : col + DH] = got_ref[first, 0:128].T
            out_ref[:, col + DH : col + 2 * DH] = got_ref[second, 0:128].T
            m1, l1 = stats_of(got_ref[first, 256:272], 2)
            m2, l2 = stats_of(got_ref[second, 256:272], 2)
            top = jnp.maximum(m1, m2)
            a, b = jnp.exp2((m1 - top) * LOG2), jnp.exp2((m2 - top) * LOG2)
            total = l1 * a + l2 * b
            acc = got_ref[first, 128:256].astype(jnp.float32) * a
            acc = (acc + got_ref[second, 128:256].astype(jnp.float32) * b) / total
            out_ref[:, col + 2 * DH : col + 3 * DH] = acc.astype(jnp.bfloat16).T


def ring(x, axis):
    routes = [[(i, (i + far) % 4) for i in range(4)] for far in (1, 2, 3)]
    return [x] + [lax.ppermute(x, axis, route) for route in routes]


def shape(dims, dtype=jnp.bfloat16):
    return jax.ShapeDtypeStruct(dims, dtype)


def state(n):
    return [shape((n, 2, 128, 128), jnp.float32)] + [shape((n, 2, 8, 128), jnp.float32)] * 2


def run_lists(place, block_mask):
    return pl.pallas_call(
        lists_kernel,
        out_shape=[shape((n,), jnp.int32) for n in (FIRST_LEN, REST_LEN, HALO_LEN, HALO_LEN, 4)],
        in_specs=[SM, SM],
        out_specs=[SM] * 5,
        compiler_params=PARAMS,
        cost_estimate=pl.CostEstimate(flops=8 * 10**9, bytes_accessed=10**5, transcendentals=0),
        name="lists",
    )(place, block_mask)


def run_own(first, rest, counts, live, kv, text_rec, q, q_other):
    return pl.pallas_call(
        own_kernel,
        out_shape=state(SLAB + 1),
        in_specs=[SM] * 4 + [ANY] * 4,
        out_specs=[VM] * 3,
        scratch_shapes=[
            pltpu.VMEM((HALF + 1, REC, DH), jnp.bfloat16),
            pltpu.VMEM((SLAB + 1, QREC, DH), jnp.bfloat16),
            pltpu.VMEM((2, 768, DH), jnp.float32),
            pltpu.VMEM((2, 768, DH), jnp.bfloat16),
            pltpu.VMEM((2, 2, 8, DH), jnp.float32),
            pltpu.VMEM((2, 2, 8, DH), jnp.float32),
            pltpu.SemaphoreType.DMA((4,)),
        ],
        compiler_params=PARAMS,
        cost_estimate=pl.CostEstimate(flops=10**8, bytes_accessed=10**6, transcendentals=0),
        name="own_keys",
    )(first, rest, counts, live, kv, text_rec, q, q_other)


def run_text(live, kv, text_rec, tq):
    scratch = [pltpu.VMEM((NTQ, 768, DH), jnp.float32), pltpu.VMEM((NTQ, 768, DH), jnp.bfloat16)]
    scratch += [pltpu.VMEM((NTQ, 2, 8, DH), jnp.float32)] * 2
    return pl.pallas_call(
        text_kernel,
        out_shape=shape((2 * NTQ, 144, DH)),
        in_specs=[SM] + [VM] * 3,
        out_specs=VM,
        scratch_shapes=scratch + [pltpu.VMEM(s.shape, jnp.float32) for s in state(NTQ)],
        compiler_params=PARAMS,
        cost_estimate=pl.CostEstimate(flops=10**7, bytes_accessed=10**5, transcendentals=0),
        name="text_keys",
    )(live, kv, text_rec, tq)


def run_halo(which, queries, table, counts, from_down, from_up, acc, m, l):
    scratch = [
        pltpu.VMEM((SLAB, REC, DH), jnp.bfloat16),
        pltpu.VMEM((HALF + 1, QREC, DH), jnp.bfloat16),
        pltpu.VMEM((2, 768, DH), jnp.float32),
        pltpu.VMEM((2, 768, DH), jnp.bfloat16),
        pltpu.VMEM((2, 2, 8, DH), jnp.float32),
        pltpu.VMEM((2, 2, 8, DH), jnp.float32),
    ]
    if which == 0:
        out = shape((HALF, OREC, DH))
        scratch += [pltpu.VMEM(s.shape, jnp.float32) for s in state(HALF + 1)]
    else:
        out = state(HALF + 1)
    return pl.pallas_call(
        functools.partial(halo_kernel, which),
        out_shape=out,
        in_specs=[SM, SM] + [ANY] * 6,
        out_specs=VM if which == 0 else [VM] * 3,
        scratch_shapes=scratch + [pltpu.SemaphoreType.DMA((6,))],
        compiler_params=PARAMS,
        cost_estimate=pl.CostEstimate(flops=2 * 10**9, bytes_accessed=10**7, transcendentals=4 * 10**6),
        name="halo_keys",
    )(table, counts, from_down, from_up, queries, acc, m, l)


def local(video_q, video_k, video_v, text_q, text_k, text_v, block_mask, text_count):
    f32 = jnp.float32
    together = lax.optimization_barrier
    y, z, c = lax.axis_index("y"), lax.axis_index("z"), lax.axis_index("c")
    pair, member = z // 2, z % 2
    chips = ("z", "x")
    swap = [(0, 1), (1, 0)]

    kv_send = pl.pallas_call(
        prep_kv_kernel, out_shape=shape((16, REC, DH)), in_specs=[ANY] * 2, out_specs=VM,
        scratch_shapes=[pltpu.VMEM((BLOCK, 24 * DH), jnp.bfloat16)] * 2 + [pltpu.SemaphoreType.DMA((6,))],
        compiler_params=pltpu.CompilerParams(vmem_limit_bytes=60 << 20), name="prep_kv",
    )(video_k, video_v)
    kv = lax.all_to_all(kv_send, chips, 0, 0, tiled=True)

    text_q, text_k, text_v, block_mask, _ = together((text_q, text_k, text_v, block_mask, kv_send))
    text = jnp.stack([text_q, text_k, text_v])
    text = jnp.where(c == pair, text, lax.ppermute(text, "c", swap))
    head = lax.dynamic_slice_in_dim(text, member * DH, DH, 2)
    shared = text[:, :, 2 * DH :]
    tq = jnp.stack([head[0].T, shared[0].T])
    tq = tq.reshape(2, DH, NTQ, DH).transpose(2, 0, 1, 3).reshape(NTQ, QREC, DH)
    mine = lax.dynamic_slice_in_dim(head, c * BLOCK, BLOCK, 1)
    half = lax.dynamic_slice_in_dim(shared, c * BLOCK + member * 64, 64, 1)
    vt = half[2].T
    text_rec = jnp.concatenate(
        [mine[1], half[1], mine[2].T, jnp.concatenate([vt[:64], vt[64:]], axis=1)], axis=0
    )[None]
    live_a = jnp.clip(text_count[0] - c * BLOCK, 0, BLOCK)
    live_c = jnp.clip(text_count[0] - c * BLOCK - member * 64, 0, 64)
    lead = y == 0
    live = jnp.stack([live_a, live_c, jnp.where(lead, live_a, 0), jnp.where(lead, live_c, 0)])
    live = live.astype(jnp.int32)
    place = jnp.stack([y, c]).astype(jnp.int32)
    first, rest, halo_a, halo_b, counts = run_lists(place, block_mask)
    video_q, tq, text_rec, first, rest, halo_a, halo_b, counts = together(
        (video_q, tq, text_rec, first, rest, halo_a, halo_b, counts)
    )
    q_send = pl.pallas_call(
        prep_q_kernel, out_shape=shape((16, QREC, DH)), in_specs=[VM], out_specs=VM,
        compiler_params=PARAMS, name="prep_q",
    )(video_q)

    q_send, kv = together((q_send, kv))
    from_down = lax.ppermute(kv, "y", [(0, 1), (1, 2), (2, 3)])
    from_up = lax.ppermute(kv, "y", [(1, 0), (2, 1), (3, 2)])
    q = lax.all_to_all(q_send, chips, 0, 0, tiled=True)
    text_part = run_text(live, kv, text_rec, tq)
    here = jnp.concatenate([text_part, lax.ppermute(text_part, "c", swap)])
    q, here = together((q, here))
    q_other = lax.ppermute(q, "c", swap)
    there = lax.ppermute(here, "z", [(0, 1), (1, 0), (2, 3), (3, 2)])
    acc, m, l = run_own(first, rest, counts, live, kv, text_rec, q, q_other)
    acc, there = together((acc, there))
    heads = pl.pallas_call(
        merge_text_kernel, out_shape=shape((3 * NTQ, 144, DH)), in_specs=[SM, VM, VM], out_specs=VM,
        compiler_params=PARAMS, name="merge_text",
    )(member.astype(jnp.int32)[None], here, there)
    acc, heads = together((acc, heads))
    far = lax.ppermute(heads, "z", [(0, 2), (1, 3), (2, 0), (3, 1)])
    heads = jnp.where(c == pair, heads, far)

    partial = run_halo(0, q_other, halo_a, counts, from_down, from_up, acc, m, l)
    got = lax.ppermute(partial, "c", swap)
    acc2, m2, l2 = run_halo(1, q, halo_b, counts, from_down, from_up, acc, m, l)
    got, heads = together((got, heads))
    record = pl.pallas_call(
        merge_kernel, out_shape=shape((HALF, OREC, DH)), in_specs=[VM] * 4, out_specs=VM,
        compiler_params=PARAMS, name="merge_cores",
    )(acc2, m2, l2, got)
    back = lax.all_to_all(record, chips, 0, 0, tiled=True)
    heads, _ = together((heads, record))
    text_out = pl.pallas_call(
        final_text_kernel, out_shape=shape((TEXT, 3 * DH)), in_specs=[VM] * 4, out_specs=VM,
        compiler_params=PARAMS, name="final_text",
    )(*ring(heads, "y"))
    video_out = pl.pallas_call(
        final_kernel, out_shape=shape((BLOCK, 24 * DH)), in_specs=[VM], out_specs=VM,
        compiler_params=PARAMS, name="final",
    )(back)
    return video_out, text_out


def solution(mesh):
    grid = Mesh(mesh.devices.reshape(4, 4, 4, 2), ("y", "z", "x", "c"))
    video = P(("y", "z", "x", "c"), None)
    text = P(None, ("x", "c"))
    return jax.shard_map(
        local,
        mesh=grid,
        in_specs=(video, video, video, text, text, text, P(), P()),
        out_specs=(video, text),
        check_vma=False,
    )
```
